256 devices in a mesh: gx: 4 (over x), gy: 4 (over y), gz: 16 (over z, core).
Axes of the slice: x: 4, y: 4, z: 8, core: 2. Of those that a mesh axis runs over, the one named last changes fastest.
Arguments:
- positions: float32 [16384, 3, 128], P(('gx', 'gy', 'gz')), may hold values from 0 to 1
- charges: float32 [16384, 128], P(('gx', 'gy', 'gz')), may hold values from -0.18 to 0.18
- counts: int32 [16384], P(('gx', 'gy', 'gz')), may hold values from 1 to 128
- up_inverse: float32 [64, 64], replicated, may hold values from -0.09375 to 0.09375
- down_inverse: float32 [64, 64], replicated, may hold values from -0.09375 to 0.09375
- inner_surface: float32 [3, 64], replicated, may hold values from 0.15 to 0.85
- outer_surface: float32 [3, 64], replicated, may hold values from -1 to 2, as said below
Outputs:
- potential: float32 [16384, 128], P(('gx', 'gy', 'gz'))
The draws below stay inside these ranges and needn't reach their ends.
Inputs may be any that keep to these rules, and one draw needn't show every extreme that they name: `outer_surface`: each point lies on the boundary of the cube [-1, 2]^3.
All inputs are finite; a program needn't handle non-finite values.
Results may differ from the reference program's by a relative error of at most 0.0003.
Values sent between devices are 32-bit elements; how exact they have to be, the bound alone decides.
No kernel may reach another device: no remote copies, remote signals or barrier semaphores. Data moves between devices by JAX's collectives and lax.ppermute only.
A program may use at most 64 MiB of HBM per device.

```python
from functools import partial
import jax
import jax.numpy as jnp
import numpy as np
from jax import lax

CX = 4
CY = 4
CZ = 4
PTS = 128
TERMS = 64
LEAVES = 16384
DEVICES = 256


def draw_outer_surface(key, part):
    first_key, second_key, third_key = jax.random.split(jax.random.fold_in(key, 7), 3)
    spot = jax.random.uniform(first_key, (3, TERMS), jnp.float32, -1.0, 1.0)
    facing = jax.random.randint(second_key, (TERMS,), 0, 3)
    signed = jax.random.randint(third_key, (TERMS,), 0, 2).astype(jnp.float32) * 2.0 - 1.0
    picked = jnp.arange(3)[:, None] == facing[None, :]
    cube = jnp.where(picked, signed[None, :], spot)
    return 0.5 + 1.5 * cube


def set_ends(array, key, least, top_value):
    dims = array.shape
    place = [jax.random.randint(jax.random.fold_in(key, axis), (), 0, dims[axis]) for axis in range(len(dims))]
    array = array.at[tuple(place)].set(least)
    longest = dims.index(max(dims))
    place[longest] = (place[longest] + 1) % dims[longest]
    return array.at[tuple(place)].set(top_value)


def shard_levels(rng, shape, pieces, low, high):
    gain = 1.0
    for axis_at, blocks in pieces:
        heights = jax.random.uniform(jax.random.fold_in(jax.random.fold_in(rng, 6), axis_at), (blocks,), jnp.float32, low / len(pieces), high / len(pieces))
        gain = gain * jnp.repeat(jnp.exp(heights), shape[axis_at] // blocks).reshape((-1,) + (1,) * (len(shape) - 1 - axis_at))
    return gain


def noise(own_key, shape, scale, limit, cuts=(), kind=jnp.bfloat16):
    drawn = jax.random.normal(own_key, shape, jnp.float32) * scale
    if len(cuts) > 0:
        drawn = shard_levels(own_key, shape, cuts, -0.22, 0.18) * drawn
    return jnp.clip(drawn, min=-limit, max=limit).astype(kind)


def setup_inputs(seed: int = 0) -> dict:
    key_list = jax.random.split(jax.random.key(seed), 8)
    return {
        "positions": jnp.clip(1.0 * jax.random.uniform(key_list[0], (LEAVES, 3, PTS), jnp.float32) ** shard_levels(key_list[0], (LEAVES, 3, PTS), ((0, 256),), -0.2, 0.2), 0.0, 1.0),
        "charges": noise(key_list[1], (LEAVES, PTS), 0.03, 0.18, ((0, 256),), jnp.float32),
        "counts": set_ends(jax.random.randint(key_list[2], (LEAVES,), 1, PTS + 1), jax.random.fold_in(key_list[2], 1), 1, PTS).astype(jnp.int32),
        "up_inverse": noise(key_list[3], (TERMS, TERMS), (TERMS * TERMS) ** -0.5, 0.09375, (), jnp.float32),
        "down_inverse": noise(key_list[4], (TERMS, TERMS), (TERMS * TERMS) ** -0.5, 0.09375, (), jnp.float32),
        "inner_surface": jnp.clip(jax.random.uniform(key_list[5], (3, TERMS), jnp.float32, 0.15, 0.85), 0.15, 0.85),
        "outer_surface": draw_outer_surface(jax.random.fold_in(key_list[7], 71), 0),
    }


SOFTEN = 0.0025
EXACT_DOTS = lax.Precision.HIGHEST

def kernel(square):
    return 1.0 / jnp.sqrt(square + SOFTEN)

def leaf_blocks(function, arrays, block_size):
    leaf_count = arrays[0].shape[0]
    shaped = tuple((member.reshape((leaf_count // block_size, block_size) + member.shape[1:]) for member in arrays))
    result = lax.map(lambda members: function(*members), shaped)
    return result.reshape((leaf_count,) + result.shape[2:])

def upward(outer, position, charge):
    square = jnp.zeros((position.shape[0], outer.shape[1], position.shape[2]), jnp.float32)
    for dimension in range(3):
        spread = outer[dimension][None, :, None] - position[:, dimension, None, :]
        square = square + spread * spread
    return jnp.einsum('nij,nj->ni', kernel(square), charge, precision=EXACT_DOTS)

def downward(outer, position, weight):
    square = jnp.zeros((position.shape[0], position.shape[2], outer.shape[1]), jnp.float32)
    for dimension in range(3):
        spread = position[:, dimension, :, None] - outer[dimension][None, None, :]
        square = square + spread * spread
    return jnp.einsum('nti,ni->nt', kernel(square), weight, precision=EXACT_DOTS)

def pair_potential(target, source, shift, exclude):
    square = jnp.zeros((target.shape[0], target.shape[2], source.shape[2]), jnp.float32)
    for dimension in range(3):
        spread = target[:, dimension, :, None] - source[:, dimension, None, :] - shift[dimension]
        square = square + spread * spread
    weight = kernel(square)
    if exclude:
        weight = weight * (1.0 - jnp.eye(target.shape[2], dtype=jnp.float32))
    return jnp.einsum('nts,ns->nt', weight, source[:, 3, :], precision=EXACT_DOTS)

def allowed(parity, shift):
    return jnp.abs(jnp.floor_divide(parity + shift, 2)) <= 1

def translate(extended, inner, span_x, span_y, span_z):
    parity_x = jnp.arange(span_x, dtype=jnp.int32) % 2
    parity_y = jnp.arange(span_y, dtype=jnp.int32) % 2
    parity_z = jnp.arange(span_z, dtype=jnp.int32) % 2
    shifts_z = jnp.arange(-3, 4, dtype=jnp.int32)
    terms_count = inner.shape[1]

    def over_x(accum, shift_x):
        slab = lax.dynamic_slice_in_dim(extended, shift_x + 3, span_x, axis=0)
        okay_x = allowed(parity_x, shift_x)
        okay_z = allowed(parity_z[None, :], shifts_z[:, None])
        spread_x = inner[0][:, None] - inner[0][None, :] - shift_x.astype(jnp.float32)
        spread_z = inner[2][None, :, None] - inner[2][None, None, :] - shifts_z.astype(jnp.float32)[:, None, None]
        for shift_y in range(-3, 4):
            rows = slab[:, 3 + shift_y:3 + shift_y + span_y]
            stacked = jnp.stack([rows[:, :, 3 + shift_z:3 + shift_z + span_z] for shift_z in range(-3, 4)])
            okay_y = allowed(parity_y, shift_y)
            spread_y = inner[1][:, None] - inner[1][None, :] - float(shift_y)
            square = (spread_x * spread_x + spread_y * spread_y)[None] + spread_z * spread_z
            matrices = kernel(square)
            extent = jnp.maximum(jnp.maximum(jnp.abs(shift_x), abs(shift_y)), jnp.abs(shifts_z))
            mask = okay_x[None, :, None, None] & okay_y[None, None, :, None] & okay_z[:, None, None, :] & (extent >= 2)[:, None, None, None]
            weighted = stacked * mask[..., None].astype(jnp.float32)
            accum = accum + jnp.einsum('oxyzj,oij->xyzi', weighted, matrices, precision=EXACT_DOTS)
        return (accum, None)
    start = jnp.zeros((span_x, span_y, span_z, terms_count), jnp.float32)
    result, _ = lax.scan(over_x, start, jnp.arange(-3, 4, dtype=jnp.int32))
    return result

def box_tables():
    total_bits = DEVICES.bit_length() - 1
    bit_counts = [len(range(dimension, total_bits, 3)) for dimension in range(3)]
    corners = np.zeros((DEVICES, 3), np.int32)
    for device in range(DEVICES):
        for dimension in range(3):
            corners[device, dimension] = sum(((device >> dimension + 3 * rank & 1) << rank for rank in range(bit_counts[dimension])))
    extent = [1 << bit_counts[dimension] for dimension in range(3)]
    device_table = np.zeros(extent, np.int32)
    device_table[corners[:, 0], corners[:, 1], corners[:, 2]] = np.arange(DEVICES, dtype=np.int32)
    return (corners, device_table, extent)

def to_grid(flat, device_table, extent):
    trailing = flat.shape[1:]
    blocks = flat.reshape((DEVICES, CX, CY, CZ) + trailing)[device_table]
    permuted = (0, 3, 1, 4, 2, 5) + tuple(range(6, 6 + len(trailing)))
    return blocks.transpose(permuted).reshape((extent[0] * CX, extent[1] * CY, extent[2] * CZ) + trailing)

def from_grid(grid, corners, extent):
    trailing = grid.shape[3:]
    shaped = grid.reshape((extent[0], CX, extent[1], CY, extent[2], CZ) + trailing)
    permuted = (0, 2, 4, 1, 3, 5) + tuple(range(6, 6 + len(trailing)))
    shaped = shaped.transpose(permuted)
    blocks = shaped[corners[:, 0], corners[:, 1], corners[:, 2]]
    return blocks.reshape((DEVICES * CX * CY * CZ,) + trailing)

def reference(positions, charges, counts, up_inverse, down_inverse, inner_surface, outer_surface):
    live = (jnp.arange(PTS, dtype=jnp.int32)[None, :] < counts[:, None]).astype(jnp.float32)
    source = charges * live
    check_up = leaf_blocks(partial(upward, outer_surface), (positions, source), 64)
    density = jnp.dot(check_up, up_inverse.T, preferred_element_type=jnp.float32, precision=EXACT_DOTS)
    corners, device_table, extent = box_tables()
    grid_x, grid_y, grid_z = (extent[0] * CX, extent[1] * CY, extent[2] * CZ)
    cell_total = grid_x * grid_y * grid_z
    dens_grid = to_grid(density, device_table, extent)
    point_grid = to_grid(jnp.concatenate([positions, source[:, None, :]], axis=1), device_table, extent)
    targets = point_grid[:, :, :, :3].reshape(cell_total, 3, PTS)
    padded = jnp.pad(point_grid, ((1, 1), (1, 1), (1, 1), (0, 0), (0, 0)))
    near = jnp.zeros((cell_total, PTS), jnp.float32)
    for shift_x in range(-1, 2):
        for shift_y in range(-1, 2):
            for shift_z in range(-1, 2):
                window = padded[1 + shift_x:1 + shift_x + grid_x, 1 + shift_y:1 + shift_y + grid_y, 1 + shift_z:1 + shift_z + grid_z]
                window = window.reshape(cell_total, 4, PTS)
                exclude = shift_x == 0 and shift_y == 0 and (shift_z == 0)
                near = near + leaf_blocks(partial(pair_potential, shift=(shift_x, shift_y, shift_z), exclude=exclude), (targets, window), 64)
    near = from_grid(near.reshape(grid_x, grid_y, grid_z, PTS), corners, extent)
    extended = jnp.pad(dens_grid, ((3, 3), (3, 3), (3, 3), (0, 0)))
    check_down = translate(extended, inner_surface, grid_x, grid_y, grid_z)
    check_down = from_grid(check_down, corners, extent)
    local = jnp.dot(check_down, down_inverse.T, preferred_element_type=jnp.float32, precision=EXACT_DOTS)
    far = leaf_blocks(partial(downward, outer_surface), (positions, local), 64)
    return live * (near + far)
```

```python
import jax
import jax.numpy as jnp
from jax import lax
from jax.experimental import pallas as pl
from jax.experimental.pallas import tpu as pltpu
from jax.sharding import PartitionSpec as P

SOFTEN = 0.0025
HIGH = lax.Precision.HIGHEST
AXES = ("gx", "gy", "gz")
BITS = ((0, 3, 6), (1, 4, 7), (2, 5))
EXTENT = (8, 8, 4)
F32 = jnp.float32
BF16 = jnp.bfloat16
VMEM = pltpu.VMEM
SMEM = pltpu.SMEM
X_ROWS = 88
Y_ROWS = 136
Z_ROWS = 224


def place(q):
    return [sum(((q >> b) & 1) << k for k, b in enumerate(BITS[d])) for d in range(3)]


def linear(c):
    return sum(((c[d] >> k) & 1) << b for d in range(3) for k, b in enumerate(BITS[d]))


def shifted(dimension, step):
    pairs = []
    for q in range(256):
        c = place(q)
        c[dimension] = (c[dimension] + step) % EXTENT[dimension]
        pairs.append((q, linear(c)))
    return pairs


def lanes(shape):
    return lax.broadcasted_iota(jnp.int32, shape, len(shape) - 1)


def point_rows(pos, n):
    return jnp.concatenate([pos[d, pl.ds(n, 1), :] for d in range(3)], axis=0)


def dot(a, b):
    return jnp.dot(a, b, precision=HIGH, preferred_element_type=F32)


def upward_kernel(counts, pos, charges, outer, up_inv, own, xup, xdn, outer_b, source, density):
    oc = jnp.transpose(jnp.concatenate([outer[...], jnp.zeros((5, 64), F32)], axis=0))
    for d in range(3):
        outer_b[d] = jnp.broadcast_to(oc[:, d : d + 1], (64, 128))
    lane = lanes((1, 128))
    lane8 = lanes((64, 128))

    def one(n, check):
        p = point_rows(pos, n)
        q = jnp.where(lane < counts[n], charges[pl.ds(n, 1), :], 0.0)
        source[pl.ds(n, 1), :] = q
        square = SOFTEN
        for d in range(3):
            spread = outer_b[d] - p[d : d + 1]
            square = square + spread * spread
        col = jnp.sum(lax.rsqrt(square) * q, axis=1, keepdims=True)
        return jnp.where(lane8 == n, col, check)

    check = lax.fori_loop(0, 64, one, jnp.zeros((64, 128), F32), unroll=4)
    dens = dot(up_inv[...], check)
    density[...] = jnp.transpose(jnp.concatenate([dens, jnp.zeros((64, 128), F32)], axis=0))
    for hz in range(2):
        even = density[pl.ds(2 * hz, 16, stride=4), :]
        odd = density[pl.ds(2 * hz + 1, 16, stride=4), :]
        own[pl.ds(16 * hz, 16), :] = jnp.where(lane < 64, even, pltpu.roll(odd, 64, 1))
    for msg, x, xl in ((xup, 3, 2), (xdn, 0, 0)):
        for hz in range(2):
            msg[pl.ds(8 * hz, 8), :] = own[pl.ds(16 * hz + 4 * xl, 8), :]
        row = jnp.zeros((1, 128), F32)
        for k in range(16):
            n = 16 * x + k
            msg[pl.ds(16 + 4 * k, 3), :] = point_rows(pos, n)
            msg[pl.ds(16 + 4 * k + 3, 1), :] = source[pl.ds(n, 1), :]
            row = jnp.where(lane == k, counts[n].astype(F32), row)
        msg[pl.ds(80, 8), :] = jnp.broadcast_to(row, (8, 128))


def upward(counts, pos, charges, outer, up_inv):
    return pl.pallas_call(
        upward_kernel,
        out_shape=(
            jax.ShapeDtypeStruct((32, 128), F32),
            jax.ShapeDtypeStruct((X_ROWS, 128), F32),
            jax.ShapeDtypeStruct((X_ROWS, 128), F32),
        ),
        in_specs=[pl.BlockSpec(memory_space=SMEM)] + [pl.BlockSpec(memory_space=VMEM)] * 4,
        scratch_shapes=[VMEM((3, 64, 128), F32), VMEM((64, 128), F32), VMEM((128, 128), F32)],
        name="upward",
    )(counts, pos, charges, outer, up_inv)


def own_points(msg, at, pos, charges, counts, n):
    msg[pl.ds(at, 3), :] = point_rows(pos, n)
    msg[pl.ds(at + 3, 1), :] = jnp.where(lanes((1, 128)) < counts[n], charges[pl.ds(n, 1), :], 0.0)


def pack_y_kernel(counts, pos, charges, own, xlo, xhi, near, yup, ydn):
    lane = lanes((1, 128))
    row = jnp.zeros((1, 128), F32)
    for k in range(64):
        row = jnp.where(lane == k, counts[k].astype(F32), row)
    for msg, y, yl in ((yup, 3, 2), (ydn, 0, 0)):
        for hz in range(2):
            for ex in range(8):
                at = pl.ds((hz * 8 + ex) * 2, 2)
                if ex < 2:
                    msg[at, :] = xlo[pl.ds((hz * 2 + ex) * 4 + yl, 2), :]
                elif ex < 6:
                    msg[at, :] = own[pl.ds((hz * 4 + ex - 2) * 4 + yl, 2), :]
                else:
                    msg[at, :] = xhi[pl.ds((hz * 2 + ex - 6) * 4 + yl, 2), :]
        for z in range(4):
            msg[pl.ds(32 + 4 * z, 4), :] = xlo[pl.ds(16 + 4 * (4 * y + z), 4), :]
            for x in range(4):
                own_points(msg, 32 + 4 * (4 * (x + 1) + z), pos, charges, counts, 16 * x + 4 * y + z)
            msg[pl.ds(32 + 4 * (20 + z), 4), :] = xhi[pl.ds(16 + 4 * (4 * y + z), 4), :]
        msg[pl.ds(128, 1), :] = row
        msg[pl.ds(129, 1), :] = xlo[pl.ds(80, 1), :]
        msg[pl.ds(130, 1), :] = xhi[pl.ds(80, 1), :]
        msg[pl.ds(131, 5), :] = jnp.zeros((5, 128), F32)


def pack_y(counts, pos, charges, own, xlo, xhi, near):
    return pl.pallas_call(
        pack_y_kernel,
        out_shape=(jax.ShapeDtypeStruct((Y_ROWS, 128), F32),) * 2,
        in_specs=[pl.BlockSpec(memory_space=SMEM)] + [pl.BlockSpec(memory_space=VMEM)] * 5 + [pl.BlockSpec(memory_space=pl.ANY)],
        name="pack_y",
    )(counts, pos, charges, own, xlo, xhi, near)


def pack_z_kernel(counts, pos, charges, own, xlo, xhi, yup, ylo, yhi, near, zup, zdn):
    for msg, z, hz in ((zup, 3, 1), (zdn, 0, 0)):
        for ex in range(8):
            at = ex * 8
            msg[pl.ds(at, 2), :] = ylo[pl.ds((hz * 8 + ex) * 2, 2), :]
            if ex < 2:
                msg[pl.ds(at + 2, 4), :] = xlo[pl.ds((hz * 2 + ex) * 4, 4), :]
            elif ex < 6:
                msg[pl.ds(at + 2, 4), :] = own[pl.ds((hz * 4 + ex - 2) * 4, 4), :]
            else:
                msg[pl.ds(at + 2, 4), :] = xhi[pl.ds((hz * 2 + ex - 6) * 4, 4), :]
            msg[pl.ds(at + 6, 2), :] = yhi[pl.ds((hz * 8 + ex) * 2, 2), :]
        for ex in range(6):
            for ey in range(6):
                at = 64 + 4 * (6 * ex + ey)
                if ey == 0:
                    msg[pl.ds(at, 4), :] = ylo[pl.ds(32 + 4 * (4 * ex + z), 4), :]
                elif ey == 5:
                    msg[pl.ds(at, 4), :] = yhi[pl.ds(32 + 4 * (4 * ex + z), 4), :]
                elif ex == 0:
                    msg[pl.ds(at, 4), :] = xlo[pl.ds(16 + 4 * (4 * (ey - 1) + z), 4), :]
                elif ex == 5:
                    msg[pl.ds(at, 4), :] = xhi[pl.ds(16 + 4 * (4 * (ey - 1) + z), 4), :]
                else:
                    own_points(msg, at, pos, charges, counts, 16 * (ex - 1) + 4 * (ey - 1) + z)
        msg[pl.ds(208, 3), :] = yup[pl.ds(128, 3), :]
        msg[pl.ds(211, 3), :] = ylo[pl.ds(128, 3), :]
        msg[pl.ds(214, 3), :] = yhi[pl.ds(128, 3), :]
        msg[pl.ds(217, 7), :] = jnp.zeros((7, 128), F32)


def pack_z(counts, pos, charges, own, xlo, xhi, yup, ylo, yhi, near):
    return pl.pallas_call(
        pack_z_kernel,
        out_shape=(jax.ShapeDtypeStruct((Z_ROWS, 128), F32),) * 2,
        in_specs=[pl.BlockSpec(memory_space=SMEM)] + [pl.BlockSpec(memory_space=VMEM)] * 8 + [pl.BlockSpec(memory_space=pl.ANY)],
        name="pack_z",
    )(counts, pos, charges, own, xlo, xhi, yup, ylo, yhi, near)


def add_source(packed, base, place_at, leaf, count, cell, lane):
    off = jnp.bitwise_and(place_at, 127)
    tile = base + jnp.right_shift(place_at, 7)
    row = lax.broadcasted_iota(jnp.int32, (4, 128), 0)
    shift = jnp.where(row == 0, cell[0], jnp.where(row == 1, cell[1], jnp.where(row == 2, cell[2], 0.0)))
    rolled = pltpu.roll(leaf + shift, off, 1)
    packed[tile, pl.ds(0, 4), :] = jnp.where(lane >= off, rolled, packed[tile, pl.ds(0, 4), :])
    packed[tile + 1, pl.ds(0, 4), :] = rolled
    return place_at + count


def close_list(packed, base, end):
    packed[base + jnp.right_shift(end, 7) + 1, pl.ds(0, 4), :] = jnp.zeros((4, 128), F32)
    packed[base + jnp.right_shift(end, 7) + 2, pl.ds(0, 4), :] = jnp.zeros((4, 128), F32)


def cell_of(n):
    return jnp.right_shift(n, 4), jnp.bitwise_and(jnp.right_shift(n, 2), 3), jnp.bitwise_and(n, 3)


def spread_targets(pos, spread, leaf_of, leaves):
    row = lax.broadcasted_iota(jnp.int32, (8, 128), 0)

    def one(i, carry):
        n = leaf_of(i)
        x, y, z = [c.astype(F32) for c in cell_of(n)]
        shift = jnp.where(row == 0, x, jnp.where(row == 1, y, z))
        flat = jnp.concatenate([point_rows(pos, n), jnp.zeros((5, 128), F32)], axis=0) + shift
        turned = jnp.transpose(flat)
        for d in range(3):
            spread[i, d] = jnp.broadcast_to(turned[:, d : d + 1], (128, 128))
        return carry

    lax.fori_loop(0, leaves, one, 0, unroll=4)


def near_sums(i, count, spread, sums, packed, segments):
    lane = lanes((1, 128))
    tiles, starts, stops, upto = [], [], [], []
    have = jnp.int32(0)
    for base, start, stop in segments:
        first = jnp.right_shift(start, 7)
        number = jnp.where(stop > start, jnp.right_shift(stop + 127, 7) - first, 0)
        tiles.append(base + first - have)
        starts.append(base * 128 + start)
        stops.append(base * 128 + stop)
        have = have + number
        upto.append(have)

    def pick(values, j):
        value = values[-1]
        for k in range(len(values) - 2, -1, -1):
            value = jnp.where(j < upto[k], values[k], value)
        return value

    def run(groups, together):
        rows = pl.ds(0, 8 * groups)
        blocks = lax.div(have + together - 1, together)

        def ahead(b):
            squares, charges = [], []
            for u in range(together):
                j = b * together + u
                tile = pick(tiles, j) + jnp.minimum(j, have - 1)
                at = tile * 128 + lane
                keep = (at >= pick(starts, j)) & (at < jnp.where(j < have, pick(stops, j), 0))
                charges.append(jnp.where(keep, packed[tile, pl.ds(3, 1), :], 0.0))
                square = SOFTEN
                for d in range(3):
                    gap = spread[i, d, rows, :] - packed[tile, pl.ds(d, 1), :]
                    square = square + gap * gap
                squares.append(square)
            return squares, charges

        def add(acc, squares, charges):
            for square, charge in zip(squares, charges):
                acc = acc + lax.rsqrt(square) * charge
            return acc

        def step(b, carry):
            acc, squares, charges = carry
            later = ahead(b)
            return (add(acc, squares, charges), *later)

        acc, squares, charges = lax.fori_loop(
            1, blocks, step, (jnp.zeros((8 * groups, 128), F32), *ahead(0))
        )
        sums[i, rows, :] = add(acc, squares, charges)

    size = jnp.right_shift(count + 31, 5)
    for k, together in ((1, 4), (2, 2), (3, 1), (4, 1)):

        @pl.when(size == k)
        def _():
            run(4 * k, together)


def gather_sums(sums, total, leaf_of, leaves):
    wide = lanes((128, 128))

    def one(i, carry):
        col = jnp.sum(sums[i], axis=1, keepdims=True)
        return jnp.where(wide == leaf_of(i), carry + col, carry)

    total[...] = lax.fori_loop(0, leaves, one, total[...], unroll=4)


def near_xy_kernel(windows, *refs):
    if len(refs) == 9:
        counts, pos, charges, total, packed, spread, sums, ends, _ = refs
        xlo = xhi = None
    else:
        counts, flags, pos, charges, xlo, xhi, before, total, packed, spread, sums, ends, lo_counts, hi_counts, sem = refs
        a = pltpu.make_async_copy(xlo.at[pl.ds(80, 1), :], lo_counts, sem.at[0])
        b = pltpu.make_async_copy(xhi.at[pl.ds(80, 1), :], hi_counts, sem.at[1])
        a.start()
        b.start()
        a.wait()
        b.wait()
    lane4 = lanes((4, 128))
    lane = lanes((1, 128))
    total[...] = jnp.zeros((128, 128), F32) if xlo is None else before[...]
    for w, x in enumerate(windows):
        for z in range(4):
            base = (w * 4 + z) * 16
            end = jnp.int32(0)
            ends[(w * 4 + z) * 5] = end
            for y in range(4):
                for dx in (-1, 0, 1):
                    sx = x + dx
                    k = 4 * y + z
                    cell = (float(sx), float(y), float(z))
                    if 0 <= sx < 4:
                        n = 16 * sx + k
                        count = counts[n]
                        q = jnp.where(lane < count, charges[pl.ds(n, 1), :], 0.0)
                        leaf = jnp.concatenate([point_rows(pos, n), q], axis=0)
                    else:
                        msg, cnt, flag = (xlo, lo_counts, 0) if sx < 0 else (xhi, hi_counts, 1)
                        count = cnt[0, k].astype(jnp.int32) * flags[flag]
                        leaf = msg[pl.ds(16 + 4 * k, 4), :]
                    end = add_source(packed, base, end, leaf, count, cell, lane4)
                ends[(w * 4 + z) * 5 + y + 1] = end
            close_list(packed, base, end)

    def leaf_of(i):
        return jnp.bitwise_and(i, 15) + 16 * (windows[0] + jnp.right_shift(i, 4) * (windows[1] - windows[0]))

    spread_targets(pos, spread, leaf_of, 32)

    def leaf_step(i, carry):
        w = jnp.right_shift(i, 4)
        n = leaf_of(i)
        x, y, z = cell_of(n)
        segments = []
        for dz in (-1, 0, 1):
            zz = jnp.clip(z + dz, 0, 3)
            lst = w * 4 + zz
            start = ends[lst * 5 + jnp.maximum(y - 1, 0)]
            stop = ends[lst * 5 + jnp.minimum(y + 1, 3) + 1]
            if dz:
                stop = jnp.where(zz == z + dz, stop, start)
            segments.append((lst * 16, start, stop))
        near_sums(i, counts[n], spread, sums, packed, segments)
        return carry

    lax.fori_loop(0, 32, leaf_step, 0)
    gather_sums(sums, total, leaf_of, 32)


def near_xy(windows, counts, pos, charges, halo=None):
    call_args = [counts, pos, charges]
    specs = [pl.BlockSpec(memory_space=SMEM)] + [pl.BlockSpec(memory_space=VMEM)] * 2
    if halo is not None:
        flags, xlo, xhi, before = halo
        call_args = [counts, flags, pos, charges, xlo, xhi, before]
        specs = [pl.BlockSpec(memory_space=SMEM)] * 2 + [pl.BlockSpec(memory_space=VMEM)] * 5
    scratch = [
        VMEM((8 * 16, 8, 128), F32),
        VMEM((32, 3, 128, 128), F32),
        VMEM((32, 128, 128), F32),
        SMEM((40,), jnp.int32),
        SMEM((1, 128), F32),
    ]
    if halo is not None:
        scratch += [SMEM((1, 128), F32), pltpu.SemaphoreType.DMA((2,))]

    def body(*refs):
        near_xy_kernel(windows, *refs)

    return pl.pallas_call(
        body,
        out_shape=jax.ShapeDtypeStruct((128, 128), F32),
        in_specs=specs,
        scratch_shapes=scratch,
        compiler_params=pltpu.CompilerParams(vmem_limit_bytes=24 * 1024 * 1024),
        cost_estimate=pl.CostEstimate(flops=150_000_000, bytes_accessed=300_000, transcendentals=10_000_000),
        name="near_x",
    )(*call_args)


def near_y_kernel(counts, flags, pos, ylo, yhi, before, total, packed, spread, sums, ends, row_counts, sem):
    copies = [
        pltpu.make_async_copy(msg.at[pl.ds(128, 8), :], row_counts.at[i], sem.at[i])
        for i, msg in enumerate((ylo, yhi))
    ]
    for c in copies:
        c.start()
    for c in copies:
        c.wait()
    lane4 = lanes((4, 128))
    total[...] = before[...]
    for side, msg in enumerate((ylo, yhi)):
        sy = -1 if side == 0 else 4
        far_y = 3 if side == 0 else 0
        for z in range(4):
            lst = side * 4 + z
            end = jnp.int32(0)
            ends[lst * 7] = end
            for ex in range(6):
                if ex == 0:
                    count = row_counts[side, 1, 4 * far_y + z].astype(jnp.int32) * flags[0]
                elif ex == 5:
                    count = row_counts[side, 2, 4 * far_y + z].astype(jnp.int32) * flags[1]
                else:
                    count = row_counts[side, 0, 16 * (ex - 1) + 4 * far_y + z].astype(jnp.int32)
                count = count * flags[2 + side]
                leaf = msg[pl.ds(32 + 4 * (4 * ex + z), 4), :]
                end = add_source(packed, lst * 10, end, leaf, count, (float(ex - 1), float(sy), float(z)), lane4)
                ends[lst * 7 + ex + 1] = end
            close_list(packed, lst * 10, end)

    def leaf_of(i):
        side = jnp.right_shift(i, 4)
        x = jnp.bitwise_and(jnp.right_shift(i, 2), 3)
        return 16 * x + 12 * side + jnp.bitwise_and(i, 3)

    spread_targets(pos, spread, leaf_of, 32)

    def leaf_step(i, carry):
        side = jnp.right_shift(i, 4)
        n = leaf_of(i)
        x, y, z = cell_of(n)
        segments = []
        for dz in (-1, 0, 1):
            zz = jnp.clip(z + dz, 0, 3)
            lst = side * 4 + zz
            start = ends[lst * 7 + x]
            stop = ends[lst * 7 + x + 3]
            if dz:
                stop = jnp.where(zz == z + dz, stop, start)
            segments.append((lst * 10, start, stop))
        near_sums(i, counts[n], spread, sums, packed, segments)
        return carry

    lax.fori_loop(0, 32, leaf_step, 0)
    gather_sums(sums, total, leaf_of, 32)


def near_y(counts, flags, pos, ylo, yhi, before):
    return pl.pallas_call(
        near_y_kernel,
        out_shape=jax.ShapeDtypeStruct((128, 128), F32),
        in_specs=[pl.BlockSpec(memory_space=SMEM)] * 2 + [pl.BlockSpec(memory_space=VMEM)] * 4,
        scratch_shapes=[
            VMEM((8 * 10, 8, 128), F32),
            VMEM((32, 3, 128, 128), F32),
            VMEM((32, 128, 128), F32),
            SMEM((56,), jnp.int32),
            SMEM((2, 8, 128), F32),
            pltpu.SemaphoreType.DMA((2,)),
        ],
        compiler_params=pltpu.CompilerParams(vmem_limit_bytes=24 * 1024 * 1024),
        cost_estimate=pl.CostEstimate(flops=60_000_000, bytes_accessed=300_000, transcendentals=4_000_000),
        name="near_y",
    )(counts, flags, pos, ylo, yhi, before)


def final_kernel(
    counts, flags, pos, charges, zup, zdn, zlo, zhi, before, inner, outer, down_inv,
    out, packed, spread, sums, ends, row_counts, total, grid, weights, left, local, sem,
):
    copies = [
        pltpu.make_async_copy(msg.at[pl.ds(208, 16), :], row_counts.at[i], sem.at[i])
        for i, msg in enumerate((zlo, zhi))
    ]
    for c in copies:
        c.start()
    grid[1] = zdn[pl.ds(0, 64), :].reshape(8, 8, 128)
    grid[2] = zup[pl.ds(0, 64), :].reshape(8, 8, 128)
    grid[0] = zlo[pl.ds(0, 64), :].reshape(8, 8, 128)
    grid[3] = zhi[pl.ds(0, 64), :].reshape(8, 8, 128)

    @pl.when(flags[0] == 0)
    def _():
        grid[:, pl.ds(0, 2)] = jnp.zeros((4, 2, 8, 128), F32)

    @pl.when(flags[1] == 0)
    def _():
        grid[:, pl.ds(6, 2)] = jnp.zeros((4, 2, 8, 128), F32)

    @pl.when(flags[2] == 0)
    def _():
        grid[:, :, pl.ds(0, 2), :] = jnp.zeros((4, 8, 2, 128), F32)

    @pl.when(flags[3] == 0)
    def _():
        grid[:, :, pl.ds(6, 2), :] = jnp.zeros((4, 8, 2, 128), F32)

    @pl.when(flags[4] == 0)
    def _():
        grid[0] = jnp.zeros((8, 8, 128), F32)

    @pl.when(flags[5] == 0)
    def _():
        grid[3] = jnp.zeros((8, 8, 128), F32)

    odd_row = jnp.bitwise_and(lax.broadcasted_iota(jnp.int32, (8, 128), 0), 1) == 1
    for oy in range(7):
        for x in range(8):
            for hb in range(3):
                begin = min(max(oy - 1, 0), 4)
                both = jnp.concatenate(
                    [grid[hb, x, pl.ds(begin, 4), :], grid[hb + 1, x, pl.ds(begin, 4), :]], axis=0
                )
                if oy == 0:
                    both = jnp.where(odd_row, pltpu.roll(both, 1, 0), 0.0)
                elif oy == 6:
                    both = jnp.where(odd_row, 0.0, pltpu.roll(both, 7, 0))
                first = both.astype(BF16)
                left[0, x, :, pl.ds(oy * 384 + hb * 128, 128)] = first.astype(F32)
                left[1, x, :, pl.ds(oy * 384 + hb * 128, 128)] = both - first.astype(F32)

    inner_rows = jnp.concatenate([inner[...], jnp.zeros((5, 64), F32)], axis=0)
    inner_cols = jnp.transpose(inner_rows)
    diff = [
        jnp.concatenate([inner[d : d + 1, :], inner[d : d + 1, :]], axis=1) - jnp.broadcast_to(inner_cols[:, d : d + 1], (64, 128))
        for d in range(3)
    ]
    wide = lanes((64, 128))
    right = jnp.where(wide >= 64, 1.0, 0.0)
    zsq = []
    for sz in range(6):
        offset = float(sz - 2) - right
        gap = diff[2] - offset
        zsq.append(gap * gap + SOFTEN)
    check = [None] * 4

    def over_x(ox, xs, rows):
        gap_x = diff[0] - float(ox)
        xsq = gap_x * gap_x
        for oy in range(-3, 4):
            gap_y = diff[1] - float(oy)
            xysq = xsq + gap_y * gap_y
            for sz in range(6):
                value = lax.rsqrt(xysq + zsq[sz])
                if max(abs(ox), abs(oy)) < 2:
                    left_near = abs(sz - 2) < 2
                    right_near = abs(sz - 3) < 2
                    if left_near:
                        value = jnp.where(wide < 64, 0.0, value)
                    if right_near:
                        value = jnp.where(wide >= 64, 0.0, value)
                first = value.astype(BF16)
                at = pl.ds((oy + 3) * 384 + sz * 64, 64)
                weights[at, pl.ds(0, 128)] = first
                weights[at, pl.ds(128, 128)] = (value - first.astype(F32)).astype(BF16)
        m = 8 * len(xs)
        lhs = jnp.concatenate([left[p, x] for p in range(2) for x in rows], axis=0).astype(BF16)
        prod = jnp.dot(lhs, weights[...], preferred_element_type=F32)
        part = prod[:m, :128] + prod[:m, 128:] + prod[m:, :128]
        for i, x in enumerate(xs):
            piece = part[8 * i : 8 * i + 8]
            check[x] = piece if check[x] is None else check[x] + piece

    for ox in range(-3, 4):
        if ox == -3:
            xs = (1, 3)
        elif ox == 3:
            xs = (0, 2)
        else:
            xs = (0, 1, 2, 3)
        over_x(ox, xs, [x + ox + 2 for x in xs])
    down = check_to_local(jnp.concatenate(check, axis=0), down_inv)
    local[...] = down

    for c in copies:
        c.wait()
    lane4 = lanes((4, 128))
    total[...] = before[...]
    for side, msg in enumerate((zlo, zhi)):
        sz = -1 if side == 0 else 4
        far_z = 3 if side == 0 else 0
        for ey in range(6):
            lst = side * 6 + ey
            end = jnp.int32(0)
            ends[lst * 7] = end
            for ex in range(6):
                group = 3 if ey == 0 else (6 if ey == 5 else 0)
                y = 3 if ey == 0 else (0 if ey == 5 else ey - 1)
                if ex == 0:
                    count = row_counts[side, group + 1, 4 * y + far_z].astype(jnp.int32) * flags[0]
                elif ex == 5:
                    count = row_counts[side, group + 2, 4 * y + far_z].astype(jnp.int32) * flags[1]
                else:
                    count = row_counts[side, group, 16 * (ex - 1) + 4 * y + far_z].astype(jnp.int32)
                if ey == 0:
                    count = count * flags[2]
                elif ey == 5:
                    count = count * flags[3]
                count = count * flags[4 + side]
                leaf = msg[pl.ds(64 + 4 * (6 * ex + ey), 4), :]
                end = add_source(packed, lst * 10, end, leaf, count, (float(ex - 1), float(ey - 1), float(sz)), lane4)
                ends[lst * 7 + ex + 1] = end
            close_list(packed, lst * 10, end)

    outer_twice = jnp.concatenate([outer[...], outer[...]], axis=1)
    lane = lanes((1, 128))

    def far_source(n, carry):
        x, y, z = cell_of(n)
        for d, c in enumerate((x, y, z)):
            packed[120 + n, pl.ds(d, 1), :] = outer_twice[d : d + 1] + c.astype(F32)
        weight = local[pl.ds(x * 8 + jnp.right_shift(z, 1) * 4 + y, 1), :]
        mine = jnp.right_shift(lane, 6) == jnp.bitwise_and(z, 1)
        packed[120 + n, pl.ds(3, 1), :] = jnp.where(mine, weight, 0.0)
        return carry

    lax.fori_loop(0, 64, far_source, 0, unroll=8)
    spread_targets(pos, spread, lambda i: i, 64)

    def leaf_step(n, carry):
        x, y, z = cell_of(n)
        side = jnp.right_shift(z, 1)
        edge = (z == 0) | (z == 3)
        segments = [(120 + n, jnp.int32(0), jnp.int32(128))]
        for dy in range(3):
            lst = side * 6 + y + dy
            start = ends[lst * 7 + x]
            stop = jnp.where(edge, ends[lst * 7 + x + 3], start)
            segments.append((lst * 10, start, stop))
        near_sums(n, counts[n], spread, sums, packed, segments)
        return carry

    lax.fori_loop(0, 64, leaf_step, 0)
    gather_sums(sums, total, lambda i: i, 64)
    both = jnp.transpose(total[...])
    row = lax.broadcasted_iota(jnp.int32, (64, 1), 0)
    full = jnp.zeros((64, 1), jnp.int32)
    for n in range(64):
        full = jnp.where(row == n, counts[n], full)
    live = lanes((64, 128)) < full
    own_term = lax.rsqrt(jnp.full((64, 128), SOFTEN, F32))
    out[...] = jnp.where(live, both[:64] - own_term * charges[...], 0.0)


def check_to_local(check, down_inv):
    flat = jnp.transpose(down_inv[...])
    zero = jnp.zeros((64, 64), F32)
    block = jnp.concatenate(
        [jnp.concatenate([flat, zero], axis=1), jnp.concatenate([zero, flat], axis=1)], axis=0
    )
    return dot(check, block)


def final(counts, flags, pos, charges, zup, zdn, zlo, zhi, before, inner, outer, down_inv):
    return pl.pallas_call(
        final_kernel,
        out_shape=jax.ShapeDtypeStruct((64, 128), F32),
        in_specs=[pl.BlockSpec(memory_space=SMEM)] * 2 + [pl.BlockSpec(memory_space=VMEM)] * 10,
        scratch_shapes=[
            VMEM((12 * 10 + 64, 8, 128), F32),
            VMEM((64, 3, 128, 128), F32),
            VMEM((64, 128, 128), F32),
            SMEM((84,), jnp.int32),
            SMEM((2, 16, 128), F32),
            VMEM((128, 128), F32),
            VMEM((4, 8, 8, 128), F32),
            VMEM((2688, 256), BF16),
            VMEM((2, 8, 8, 2688), F32),
            VMEM((32, 128), F32),
            pltpu.SemaphoreType.DMA((2,)),
        ],
        compiler_params=pltpu.CompilerParams(vmem_limit_bytes=56 * 1024 * 1024),
        name="final",
    )(counts, flags, pos, charges, zup, zdn, zlo, zhi, before, inner, outer, down_inv)


def exchange(up, down, dimension):
    return (
        lax.ppermute(up, AXES, shifted(dimension, 1)),
        lax.ppermute(down, AXES, shifted(dimension, -1)),
    )


def per_device(positions, charges, counts, up_inverse, down_inverse, inner_surface, outer_surface):
    device = (lax.axis_index("gx") * 4 + lax.axis_index("gy")) * 16 + lax.axis_index("gz")
    sides = []
    for d in range(3):
        at = jnp.zeros((), jnp.int32)
        for k, b in enumerate(BITS[d]):
            at = at + jnp.left_shift(jnp.bitwise_and(jnp.right_shift(device, b), 1), k)
        sides += [at > 0, at < EXTENT[d] - 1]
    flags = jnp.stack(sides).astype(jnp.int32)
    positions = jnp.transpose(positions, (1, 0, 2))
    own, xup, xdn = upward(counts, positions, charges, outer_surface, up_inverse)
    xlo, xhi = exchange(xup, xdn, 0)
    near = near_xy((1, 2), counts, positions, charges)
    yup, ydn = pack_y(counts, positions, charges, own, xlo, xhi, near)
    ylo, yhi = exchange(yup, ydn, 1)
    near = near_xy((0, 3), counts, positions, charges, (flags, xlo, xhi, near))
    zup, zdn = pack_z(counts, positions, charges, own, xlo, xhi, yup, ylo, yhi, near)
    zlo, zhi = exchange(zup, zdn, 2)
    near = near_y(counts, flags, positions, ylo, yhi, near)
    return final(
        counts, flags, positions, charges, zup, zdn, zlo, zhi, near, inner_surface, outer_surface, down_inverse
    )


def solution(mesh):
    split = AXES
    return jax.shard_map(
        per_device,
        mesh=mesh,
        in_specs=(P(split, None, None), P(split, None), P(split), P(), P(), P(), P()),
        out_specs=P(split, None),
        check_vma=False,
    )
```

```python
import jax
import jax.numpy as jnp
from jax import lax
from jax.experimental import pallas as pl
from jax.experimental.pallas import tpu as pltpu
from jax.sharding import PartitionSpec as P

SOFTEN = 0.0025
HIGH = lax.Precision.HIGHEST
AXES = ("gx", "gy", "gz")
BITS = ((0, 3, 6), (1, 4, 7), (2, 5))
EXTENT = (8, 8, 4)
F32 = jnp.float32
BF16 = jnp.bfloat16
VMEM = pltpu.VMEM
SMEM = pltpu.SMEM
X_ROWS = 88
Y_ROWS = 136
Z_ROWS = 224


def place(q):
    return [sum(((q >> b) & 1) << k for k, b in enumerate(BITS[d])) for d in range(3)]


def linear(c):
    return sum(((c[d] >> k) & 1) << b for d in range(3) for k, b in enumerate(BITS[d]))


def shifted(dimension, step):
    pairs = []
    for q in range(256):
        c = place(q)
        c[dimension] = (c[dimension] + step) % EXTENT[dimension]
        pairs.append((q, linear(c)))
    return pairs


def lanes(shape):
    return lax.broadcasted_iota(jnp.int32, shape, len(shape) - 1)


def point_rows(pos, n):
    return jnp.concatenate([pos[d, pl.ds(n, 1), :] for d in range(3)], axis=0)


def dot(a, b):
    return jnp.dot(a, b, precision=HIGH, preferred_element_type=F32)


def lane_sums(value):
    return jnp.sum(jnp.transpose(value), axis=0, keepdims=True)


TOGETHER_LEAVES = 4


def by_fours(leaves, load, work, store):
    def step(k, carry):
        at = [k * TOGETHER_LEAVES + u for u in range(TOGETHER_LEAVES)]
        loaded = [load(i) for i in at]
        made = [work(*value) for value in loaded]
        for i, value in zip(at, made):
            store(i, value)
        return carry

    lax.fori_loop(0, leaves // TOGETHER_LEAVES, step, 0)


def upward_kernel(counts, pos, charges, outer, up_inv, own, xup, xdn, outer_b, source, density, check):
    oc = jnp.transpose(jnp.concatenate([outer[...], jnp.zeros((5, 64), F32)], axis=0))
    for d in range(3):
        outer_b[d] = jnp.broadcast_to(oc[:, d : d + 1], (64, 128))
    lane = lanes((1, 128))

    def load(n):
        return point_rows(pos, n), charges[pl.ds(n, 1), :], counts[n]

    def work(p, charge, count):
        q = jnp.where(lane < count, charge, 0.0)
        square = SOFTEN
        for d in range(3):
            spread = outer_b[d] - p[d : d + 1]
            square = square + spread * spread
        return q, lane_sums(lax.rsqrt(square) * q)

    def store(n, value):
        source[pl.ds(n, 1), :] = value[0]
        check[pl.ds(n, 1), :] = value[1]

    by_fours(64, load, work, store)
    dens = lax.dot_general(
        check[...], up_inv[...], (((1,), (1,)), ((), ())), precision=HIGH, preferred_element_type=F32
    )
    density[...] = jnp.concatenate([dens, dens], axis=1)
    for hz in range(2):
        even = density[pl.ds(2 * hz, 16, stride=4), :]
        odd = density[pl.ds(2 * hz + 1, 16, stride=4), :]
        own[pl.ds(16 * hz, 16), :] = jnp.where(lane < 64, even, odd)
    for msg, x, xl in ((xup, 3, 2), (xdn, 0, 0)):
        for hz in range(2):
            msg[pl.ds(8 * hz, 8), :] = own[pl.ds(16 * hz + 4 * xl, 8), :]
        row = jnp.zeros((1, 128), F32)
        for k in range(16):
            n = 16 * x + k
            msg[pl.ds(16 + 4 * k, 3), :] = point_rows(pos, n)
            msg[pl.ds(16 + 4 * k + 3, 1), :] = source[pl.ds(n, 1), :]
            row = jnp.where(lane == k, counts[n].astype(F32), row)
        msg[pl.ds(80, 8), :] = jnp.broadcast_to(row, (8, 128))


def upward(counts, pos, charges, outer, up_inv):
    return pl.pallas_call(
        upward_kernel,
        out_shape=(
            jax.ShapeDtypeStruct((32, 128), F32),
            jax.ShapeDtypeStruct((X_ROWS, 128), F32),
            jax.ShapeDtypeStruct((X_ROWS, 128), F32),
        ),
        in_specs=[pl.BlockSpec(memory_space=SMEM)] + [pl.BlockSpec(memory_space=VMEM)] * 4,
        scratch_shapes=[VMEM((3, 64, 128), F32), VMEM((64, 128), F32), VMEM((64, 128), F32), VMEM((64, 64), F32)],
        name="upward",
    )(counts, pos, charges, outer, up_inv)


def own_points(msg, at, pos, charges, counts, n):
    msg[pl.ds(at, 3), :] = point_rows(pos, n)
    msg[pl.ds(at + 3, 1), :] = jnp.where(lanes((1, 128)) < counts[n], charges[pl.ds(n, 1), :], 0.0)


def pack_y_kernel(counts, pos, charges, own, xlo, xhi, near, yup, ydn):
    lane = lanes((1, 128))
    row = jnp.zeros((1, 128), F32)
    for k in range(64):
        row = jnp.where(lane == k, counts[k].astype(F32), row)
    for msg, y, yl in ((yup, 3, 2), (ydn, 0, 0)):
        for hz in range(2):
            for ex in range(8):
                at = pl.ds((hz * 8 + ex) * 2, 2)
                if ex < 2:
                    msg[at, :] = xlo[pl.ds((hz * 2 + ex) * 4 + yl, 2), :]
                elif ex < 6:
                    msg[at, :] = own[pl.ds((hz * 4 + ex - 2) * 4 + yl, 2), :]
                else:
                    msg[at, :] = xhi[pl.ds((hz * 2 + ex - 6) * 4 + yl, 2), :]
        for z in range(4):
            msg[pl.ds(32 + 4 * z, 4), :] = xlo[pl.ds(16 + 4 * (4 * y + z), 4), :]
            for x in range(4):
                own_points(msg, 32 + 4 * (4 * (x + 1) + z), pos, charges, counts, 16 * x + 4 * y + z)
            msg[pl.ds(32 + 4 * (20 + z), 4), :] = xhi[pl.ds(16 + 4 * (4 * y + z), 4), :]
        msg[pl.ds(128, 1), :] = row
        msg[pl.ds(129, 1), :] = xlo[pl.ds(80, 1), :]
        msg[pl.ds(130, 1), :] = xhi[pl.ds(80, 1), :]
        msg[pl.ds(131, 5), :] = jnp.zeros((5, 128), F32)


def pack_y(counts, pos, charges, own, xlo, xhi, near):
    return pl.pallas_call(
        pack_y_kernel,
        out_shape=(jax.ShapeDtypeStruct((Y_ROWS, 128), F32),) * 2,
        in_specs=[pl.BlockSpec(memory_space=SMEM)] + [pl.BlockSpec(memory_space=VMEM)] * 5 + [pl.BlockSpec(memory_space=pl.ANY)],
        compiler_params=pltpu.CompilerParams(vmem_limit_bytes=6 * 1024 * 1024),
        name="pack_y",
    )(counts, pos, charges, own, xlo, xhi, near)


def pack_z_kernel(counts, pos, charges, own, xlo, xhi, yup, ylo, yhi, near, zup, zdn):
    for msg, z, hz in ((zup, 3, 1), (zdn, 0, 0)):
        for ex in range(8):
            at = ex * 8
            msg[pl.ds(at, 2), :] = ylo[pl.ds((hz * 8 + ex) * 2, 2), :]
            if ex < 2:
                msg[pl.ds(at + 2, 4), :] = xlo[pl.ds((hz * 2 + ex) * 4, 4), :]
            elif ex < 6:
                msg[pl.ds(at + 2, 4), :] = own[pl.ds((hz * 4 + ex - 2) * 4, 4), :]
            else:
                msg[pl.ds(at + 2, 4), :] = xhi[pl.ds((hz * 2 + ex - 6) * 4, 4), :]
            msg[pl.ds(at + 6, 2), :] = yhi[pl.ds((hz * 8 + ex) * 2, 2), :]
        for ex in range(6):
            for ey in range(6):
                at = 64 + 4 * (6 * ex + ey)
                if ey == 0:
                    msg[pl.ds(at, 4), :] = ylo[pl.ds(32 + 4 * (4 * ex + z), 4), :]
                elif ey == 5:
                    msg[pl.ds(at, 4), :] = yhi[pl.ds(32 + 4 * (4 * ex + z), 4), :]
                elif ex == 0:
                    msg[pl.ds(at, 4), :] = xlo[pl.ds(16 + 4 * (4 * (ey - 1) + z), 4), :]
                elif ex == 5:
                    msg[pl.ds(at, 4), :] = xhi[pl.ds(16 + 4 * (4 * (ey - 1) + z), 4), :]
                else:
                    own_points(msg, at, pos, charges, counts, 16 * (ex - 1) + 4 * (ey - 1) + z)
        msg[pl.ds(208, 3), :] = yup[pl.ds(128, 3), :]
        msg[pl.ds(211, 3), :] = ylo[pl.ds(128, 3), :]
        msg[pl.ds(214, 3), :] = yhi[pl.ds(128, 3), :]
        msg[pl.ds(217, 7), :] = jnp.zeros((7, 128), F32)


def pack_z(counts, pos, charges, own, xlo, xhi, yup, ylo, yhi, near):
    return pl.pallas_call(
        pack_z_kernel,
        out_shape=(jax.ShapeDtypeStruct((Z_ROWS, 128), F32),) * 2,
        in_specs=[pl.BlockSpec(memory_space=SMEM)] + [pl.BlockSpec(memory_space=VMEM)] * 8 + [pl.BlockSpec(memory_space=pl.ANY)],
        compiler_params=pltpu.CompilerParams(vmem_limit_bytes=6 * 1024 * 1024),
        name="pack_z",
    )(counts, pos, charges, own, xlo, xhi, yup, ylo, yhi, near)


def add_source(packed, base, place_at, leaf, count, cell, lane):
    off = jnp.bitwise_and(place_at, 127)
    tile = base + jnp.right_shift(place_at, 7)
    row = lax.broadcasted_iota(jnp.int32, (4, 128), 0)
    shift = jnp.where(row == 0, cell[0], jnp.where(row == 1, cell[1], jnp.where(row == 2, cell[2], 0.0)))
    rolled = pltpu.roll(leaf + shift, off, 1)
    packed[tile, pl.ds(0, 4), :] = jnp.where(lane >= off, rolled, packed[tile, pl.ds(0, 4), :])
    packed[tile + 1, pl.ds(0, 4), :] = rolled
    return place_at + count


def close_list(packed, base, end):
    packed[base + jnp.right_shift(end, 7) + 1, pl.ds(0, 4), :] = jnp.zeros((4, 128), F32)
    packed[base + jnp.right_shift(end, 7) + 2, pl.ds(0, 4), :] = jnp.zeros((4, 128), F32)


def cell_of(n):
    return jnp.right_shift(n, 4), jnp.bitwise_and(jnp.right_shift(n, 2), 3), jnp.bitwise_and(n, 3)


def spread_targets(pos, spread, turned, leaf_of, leaves):
    number = lax.broadcasted_iota(jnp.int32, (64, 128), 0)
    for d, part in enumerate(cell_of(number)):
        flat = pos[d] + part.astype(F32)
        rest = jnp.transpose(jnp.concatenate([flat, flat], axis=0))[:, :64]
        for p in range(3):
            piece = rest.astype(BF16)
            turned[d, :, pl.ds(64 * p, 64)] = piece
            rest = rest - piece.astype(F32)
    place_of = jnp.bitwise_and(lax.broadcasted_iota(jnp.int32, (192, 128), 0), 63)

    def step(k, carry):
        pick = jnp.concatenate(
            [jnp.where(place_of == leaf_of(4 * k + u), 1.0, 0.0).astype(BF16) for u in range(4)], axis=1
        )
        wide = [jnp.dot(turned[d], pick, preferred_element_type=F32) for d in range(3)]
        for u in range(4):
            for d in range(3):
                spread[4 * k + u, d] = wide[d][:, 128 * u : 128 * (u + 1)]
        return carry

    lax.fori_loop(0, leaves // 4, step, 0)


TOGETHER = ((1, 4), (2, 4), (3, 3), (4, 2))


def near_sums(i, count, spread, sums, packed, segments, fresh=True):
    lane = lanes((1, 128))

    def run(groups, together):
        rows = pl.ds(0, 8 * groups)
        acc = jnp.zeros((8 * groups, 128), F32) if fresh else sums[i, rows, :]
        for base, start, stop in segments:
            first = jnp.right_shift(start, 7)
            last = jnp.right_shift(stop + 127, 7) - 1
            number = jnp.where(stop > start, last - first + 1, 0)

            def block(b, acc, first=first, last=last, start=start, stop=stop, base=base):
                for u in range(together):
                    tile = first + b * together + u
                    at = lane + tile * 128
                    where = base + jnp.minimum(tile, last)
                    charge = jnp.where((at >= start) & (at < stop), packed[where, pl.ds(3, 1), :], 0.0)
                    square = SOFTEN
                    for d in range(3):
                        gap = spread[i, d, rows, :] - packed[where, pl.ds(d, 1), :]
                        square = square + gap * gap
                    acc = acc + lax.rsqrt(square) * charge
                return acc

            acc = lax.fori_loop(0, lax.div(number + together - 1, together), block, acc)
        sums[i, rows, :] = acc

    size = jnp.right_shift(count + 31, 5)
    for k, together in TOGETHER:

        @pl.when(size == k)
        def _():
            run(4 * k, together)


def gather_sums(sums, total, leaf_of, leaves):
    wide = lanes((128, 128))
    ones = jnp.ones((256, 128), BF16)

    def step(k, carry):
        value = jnp.concatenate([sums[4 * k + u] for u in range(4)], axis=0)
        first = value.astype(BF16)
        second = (value - first.astype(F32)).astype(BF16)
        column = jnp.dot(jnp.concatenate([first, second], axis=1), ones, preferred_element_type=F32)
        for u in range(4):
            carry = jnp.where(wide == leaf_of(4 * k + u), carry + column[128 * u : 128 * (u + 1)], carry)
        return carry

    total[...] = lax.fori_loop(0, leaves // 4, step, total[...])


def near_xy_kernel(windows, *refs):
    if len(refs) == 10:
        counts, pos, charges, total, packed, spread, turned, sums, ends, _ = refs
        xlo = xhi = None
    else:
        counts, flags, pos, charges, xlo, xhi, before, total, packed, spread, turned, sums, ends, lo_counts, hi_counts, sem = refs
        a = pltpu.make_async_copy(xlo.at[pl.ds(80, 1), :], lo_counts, sem.at[0])
        b = pltpu.make_async_copy(xhi.at[pl.ds(80, 1), :], hi_counts, sem.at[1])
        a.start()
        b.start()
        a.wait()
        b.wait()
    lane4 = lanes((4, 128))
    lane = lanes((1, 128))
    total[...] = jnp.zeros((128, 128), F32) if xlo is None else before[...]
    for w, x in enumerate(windows):
        for z in range(4):
            base = (w * 4 + z) * 16
            end = jnp.int32(0)
            ends[(w * 4 + z) * 5] = end
            for y in range(4):
                for dx in (-1, 0, 1):
                    sx = x + dx
                    k = 4 * y + z
                    cell = (float(sx), float(y), float(z))
                    if 0 <= sx < 4:
                        n = 16 * sx + k
                        count = counts[n]
                        q = jnp.where(lane < count, charges[pl.ds(n, 1), :], 0.0)
                        leaf = jnp.concatenate([point_rows(pos, n), q], axis=0)
                    else:
                        msg, cnt, flag = (xlo, lo_counts, 0) if sx < 0 else (xhi, hi_counts, 1)
                        count = cnt[0, k].astype(jnp.int32) * flags[flag]
                        leaf = msg[pl.ds(16 + 4 * k, 4), :]
                    end = add_source(packed, base, end, leaf, count, cell, lane4)
                ends[(w * 4 + z) * 5 + y + 1] = end
            close_list(packed, base, end)

    def leaf_of(i):
        return jnp.bitwise_and(i, 15) + 16 * (windows[0] + jnp.right_shift(i, 4) * (windows[1] - windows[0]))

    spread_targets(pos, spread, turned, leaf_of, 32)

    def leaf_step(i, carry):
        w = jnp.right_shift(i, 4)
        n = leaf_of(i)
        x, y, z = cell_of(n)
        segments = []
        for dz in (-1, 0, 1):
            zz = jnp.clip(z + dz, 0, 3)
            lst = w * 4 + zz
            start = ends[lst * 5 + jnp.maximum(y - 1, 0)]
            stop = ends[lst * 5 + jnp.minimum(y + 1, 3) + 1]
            if dz:
                stop = jnp.where(zz == z + dz, stop, start)
            segments.append((lst * 16, start, stop))
        near_sums(i, counts[n], spread, sums, packed, segments)
        return carry

    lax.fori_loop(0, 32, leaf_step, 0)
    gather_sums(sums, total, leaf_of, 32)


def near_xy(windows, counts, pos, charges, halo=None):
    call_args = [counts, pos, charges]
    specs = [pl.BlockSpec(memory_space=SMEM)] + [pl.BlockSpec(memory_space=VMEM)] * 2
    if halo is not None:
        flags, xlo, xhi, before = halo
        call_args = [counts, flags, pos, charges, xlo, xhi, before]
        specs = [pl.BlockSpec(memory_space=SMEM)] * 2 + [pl.BlockSpec(memory_space=VMEM)] * 5
    scratch = [
        VMEM((8 * 16, 8, 128), F32),
        VMEM((32, 3, 128, 128), F32),
            VMEM((3, 128, 192), BF16),
        VMEM((32, 128, 128), F32),
        SMEM((40,), jnp.int32),
        SMEM((1, 128), F32),
    ]
    if halo is not None:
        scratch += [SMEM((1, 128), F32), pltpu.SemaphoreType.DMA((2,))]

    def body(*refs):
        near_xy_kernel(windows, *refs)

    return pl.pallas_call(
        body,
        out_shape=jax.ShapeDtypeStruct((128, 128), F32),
        in_specs=specs,
        scratch_shapes=scratch,
        compiler_params=pltpu.CompilerParams(vmem_limit_bytes=14 * 1024 * 1024),
        cost_estimate=pl.CostEstimate(flops=150_000_000, bytes_accessed=300_000, transcendentals=10_000_000),
        name="near_x",
    )(*call_args)


def near_y_kernel(counts, flags, pos, ylo, yhi, before, total, packed, spread, turned, sums, ends, row_counts, sem):
    copies = [
        pltpu.make_async_copy(msg.at[pl.ds(128, 8), :], row_counts.at[i], sem.at[i])
        for i, msg in enumerate((ylo, yhi))
    ]
    for c in copies:
        c.start()
    for c in copies:
        c.wait()
    lane4 = lanes((4, 128))
    total[...] = before[...]
    for side, msg in enumerate((ylo, yhi)):
        sy = -1 if side == 0 else 4
        far_y = 3 if side == 0 else 0
        for z in range(4):
            lst = side * 4 + z
            end = jnp.int32(0)
            ends[lst * 7] = end
            for ex in range(6):
                if ex == 0:
                    count = row_counts[side, 1, 4 * far_y + z].astype(jnp.int32) * flags[0]
                elif ex == 5:
                    count = row_counts[side, 2, 4 * far_y + z].astype(jnp.int32) * flags[1]
                else:
                    count = row_counts[side, 0, 16 * (ex - 1) + 4 * far_y + z].astype(jnp.int32)
                count = count * flags[2 + side]
                leaf = msg[pl.ds(32 + 4 * (4 * ex + z), 4), :]
                end = add_source(packed, lst * 10, end, leaf, count, (float(ex - 1), float(sy), float(z)), lane4)
                ends[lst * 7 + ex + 1] = end
            close_list(packed, lst * 10, end)

    def leaf_of(i):
        side = jnp.right_shift(i, 4)
        x = jnp.bitwise_and(jnp.right_shift(i, 2), 3)
        return 16 * x + 12 * side + jnp.bitwise_and(i, 3)

    spread_targets(pos, spread, turned, leaf_of, 32)

    def leaf_step(i, carry):
        side = jnp.right_shift(i, 4)
        n = leaf_of(i)
        x, y, z = cell_of(n)
        segments = []
        for dz in (-1, 0, 1):
            zz = jnp.clip(z + dz, 0, 3)
            lst = side * 4 + zz
            start = ends[lst * 7 + x]
            stop = ends[lst * 7 + x + 3]
            if dz:
                stop = jnp.where(zz == z + dz, stop, start)
            segments.append((lst * 10, start, stop))
        near_sums(i, counts[n], spread, sums, packed, segments)
        return carry

    lax.fori_loop(0, 32, leaf_step, 0)
    gather_sums(sums, total, leaf_of, 32)


def near_y(counts, flags, pos, ylo, yhi, before):
    return pl.pallas_call(
        near_y_kernel,
        out_shape=jax.ShapeDtypeStruct((128, 128), F32),
        in_specs=[pl.BlockSpec(memory_space=SMEM)] * 2 + [pl.BlockSpec(memory_space=VMEM)] * 4,
        scratch_shapes=[
            VMEM((8 * 10, 8, 128), F32),
            VMEM((32, 3, 128, 128), F32),
            VMEM((3, 128, 192), BF16),
            VMEM((32, 128, 128), F32),
            SMEM((56,), jnp.int32),
            SMEM((2, 8, 128), F32),
            pltpu.SemaphoreType.DMA((2,)),
        ],
        compiler_params=pltpu.CompilerParams(vmem_limit_bytes=14 * 1024 * 1024),
        cost_estimate=pl.CostEstimate(flops=60_000_000, bytes_accessed=300_000, transcendentals=4_000_000),
        name="near_y",
    )(counts, flags, pos, ylo, yhi, before)


def final_kernel(
    counts, flags, pos, charges, zup, zdn, zlo, zhi, before, inner, outer, down_inv,
    out, packed, spread, turned, sums, ends, row_counts, total, grid, weights, left, local, sem,
):
    copies = [
        pltpu.make_async_copy(msg.at[pl.ds(208, 16), :], row_counts.at[i], sem.at[i])
        for i, msg in enumerate((zlo, zhi))
    ]
    for c in copies:
        c.start()
    grid[1] = zdn[pl.ds(0, 64), :].reshape(8, 8, 128)
    grid[2] = zup[pl.ds(0, 64), :].reshape(8, 8, 128)
    grid[0] = zlo[pl.ds(0, 64), :].reshape(8, 8, 128)
    grid[3] = zhi[pl.ds(0, 64), :].reshape(8, 8, 128)

    @pl.when(flags[0] == 0)
    def _():
        grid[:, pl.ds(0, 2)] = jnp.zeros((4, 2, 8, 128), F32)

    @pl.when(flags[1] == 0)
    def _():
        grid[:, pl.ds(6, 2)] = jnp.zeros((4, 2, 8, 128), F32)

    @pl.when(flags[2] == 0)
    def _():
        grid[:, :, pl.ds(0, 2), :] = jnp.zeros((4, 8, 2, 128), F32)

    @pl.when(flags[3] == 0)
    def _():
        grid[:, :, pl.ds(6, 2), :] = jnp.zeros((4, 8, 2, 128), F32)

    @pl.when(flags[4] == 0)
    def _():
        grid[0] = jnp.zeros((8, 8, 128), F32)

    @pl.when(flags[5] == 0)
    def _():
        grid[3] = jnp.zeros((8, 8, 128), F32)

    odd_row = jnp.bitwise_and(lax.broadcasted_iota(jnp.int32, (8, 128), 0), 1) == 1
    for oy in range(7):
        for x in range(8):
            for hb in range(3):
                begin = min(max(oy - 1, 0), 4)
                both = jnp.concatenate(
                    [grid[hb, x, pl.ds(begin, 4), :], grid[hb + 1, x, pl.ds(begin, 4), :]], axis=0
                )
                if oy == 0:
                    both = jnp.where(odd_row, pltpu.roll(both, 1, 0), 0.0)
                elif oy == 6:
                    both = jnp.where(odd_row, 0.0, pltpu.roll(both, 7, 0))
                first = both.astype(BF16)
                left[0, x, :, pl.ds(oy * 384 + hb * 128, 128)] = first.astype(F32)
                left[1, x, :, pl.ds(oy * 384 + hb * 128, 128)] = both - first.astype(F32)

    inner_rows = jnp.concatenate([inner[...], jnp.zeros((5, 64), F32)], axis=0)
    inner_cols = jnp.transpose(inner_rows)
    diff = [
        jnp.concatenate([inner[d : d + 1, :], inner[d : d + 1, :]], axis=1) - jnp.broadcast_to(inner_cols[:, d : d + 1], (64, 128))
        for d in range(3)
    ]
    wide = lanes((64, 128))
    right = jnp.where(wide >= 64, 1.0, 0.0)
    zsq = []
    for sz in range(6):
        offset = float(sz - 2) - right
        gap = diff[2] - offset
        zsq.append(gap * gap + SOFTEN)
    check = [None] * 4

    def over_x(ox, xs, rows):
        gap_x = diff[0] - float(ox)
        xsq = gap_x * gap_x
        for oy in range(-3, 4):
            gap_y = diff[1] - float(oy)
            xysq = xsq + gap_y * gap_y
            for sz in range(6):
                value = lax.rsqrt(xysq + zsq[sz])
                if max(abs(ox), abs(oy)) < 2:
                    left_near = abs(sz - 2) < 2
                    right_near = abs(sz - 3) < 2
                    if left_near:
                        value = jnp.where(wide < 64, 0.0, value)
                    if right_near:
                        value = jnp.where(wide >= 64, 0.0, value)
                first = value.astype(BF16)
                at = pl.ds((oy + 3) * 384 + sz * 64, 64)
                weights[at, pl.ds(0, 128)] = first
                weights[at, pl.ds(128, 128)] = (value - first.astype(F32)).astype(BF16)
        m = 8 * len(xs)
        lhs = jnp.concatenate([left[p, x] for p in range(2) for x in rows], axis=0).astype(BF16)
        prod = jnp.dot(lhs, weights[...], preferred_element_type=F32)
        part = prod[:m, :128] + prod[:m, 128:] + prod[m:, :128]
        for i, x in enumerate(xs):
            piece = part[8 * i : 8 * i + 8]
            check[x] = piece if check[x] is None else check[x] + piece

    for ox in range(-3, 4):
        if ox == -3:
            xs = (1, 3)
        elif ox == 3:
            xs = (0, 2)
        else:
            xs = (0, 1, 2, 3)
        over_x(ox, xs, [x + ox + 2 for x in xs])
    down = check_to_local(jnp.concatenate(check, axis=0), down_inv)
    local[...] = down

    for c in copies:
        c.wait()
    lane4 = lanes((4, 128))
    total[...] = before[...]
    for side, msg in enumerate((zlo, zhi)):
        sz = -1 if side == 0 else 4
        far_z = 3 if side == 0 else 0
        for ey in range(6):
            lst = side * 6 + ey
            end = jnp.int32(0)
            ends[lst * 7] = end
            for ex in range(6):
                group = 3 if ey == 0 else (6 if ey == 5 else 0)
                y = 3 if ey == 0 else (0 if ey == 5 else ey - 1)
                if ex == 0:
                    count = row_counts[side, group + 1, 4 * y + far_z].astype(jnp.int32) * flags[0]
                elif ex == 5:
                    count = row_counts[side, group + 2, 4 * y + far_z].astype(jnp.int32) * flags[1]
                else:
                    count = row_counts[side, group, 16 * (ex - 1) + 4 * y + far_z].astype(jnp.int32)
                if ey == 0:
                    count = count * flags[2]
                elif ey == 5:
                    count = count * flags[3]
                count = count * flags[4 + side]
                leaf = msg[pl.ds(64 + 4 * (6 * ex + ey), 4), :]
                end = add_source(packed, lst * 10, end, leaf, count, (float(ex - 1), float(ey - 1), float(sz)), lane4)
                ends[lst * 7 + ex + 1] = end
            close_list(packed, lst * 10, end)

    outer_twice = jnp.concatenate([outer[...], outer[...]], axis=1)
    lane = lanes((1, 128))

    spread_targets(pos, spread, turned, lambda i: i, 64)

    def far_step(n, carry):
        cell = cell_of(n)
        x, y, z = cell
        weight = local[pl.ds(x * 8 + jnp.right_shift(z, 1) * 4 + y, 1), :]
        weight = jnp.where(jnp.right_shift(lane, 6) == jnp.bitwise_and(z, 1), weight, 0.0)
        square = SOFTEN
        for d in range(3):
            gap = spread[n, d] - (outer_twice[d : d + 1] + cell[d].astype(F32))
            square = square + gap * gap
        sums[n] = lax.rsqrt(square) * weight
        return carry

    lax.fori_loop(0, 64, far_step, 0, unroll=2)

    def leaf_step(i, carry):
        side = jnp.bitwise_and(i, 1)
        n = jnp.right_shift(i, 1) * 4 + 3 * side
        x, y, z = cell_of(n)
        segments = []
        for dy in range(3):
            lst = side * 6 + y + dy
            segments.append((lst * 10, ends[lst * 7 + x], ends[lst * 7 + x + 3]))
        near_sums(n, counts[n], spread, sums, packed, segments, fresh=False)
        return carry

    lax.fori_loop(0, 32, leaf_step, 0)
    gather_sums(sums, total, lambda i: i, 64)
    row = lax.broadcasted_iota(jnp.int32, (64, 1), 0)
    full = jnp.zeros((64, 1), jnp.int32)
    for n in range(64):
        full = jnp.where(row == n, counts[n], full)
    live = lanes((64, 128)) < full
    own_term = lax.rsqrt(jnp.full((64, 128), SOFTEN, F32))
    out[...] = jnp.where(live, jnp.transpose(total[...])[:64] - own_term * charges[...], 0.0)


def check_to_local(check, down_inv):
    flat = jnp.transpose(down_inv[...])
    zero = jnp.zeros((64, 64), F32)
    block = jnp.concatenate(
        [jnp.concatenate([flat, zero], axis=1), jnp.concatenate([zero, flat], axis=1)], axis=0
    )
    return dot(check, block)


def final(counts, flags, pos, charges, zup, zdn, zlo, zhi, before, inner, outer, down_inv):
    return pl.pallas_call(
        final_kernel,
        out_shape=jax.ShapeDtypeStruct((64, 128), F32),
        in_specs=[pl.BlockSpec(memory_space=SMEM)] * 2 + [pl.BlockSpec(memory_space=VMEM)] * 10,
        scratch_shapes=[
            VMEM((12 * 10, 8, 128), F32),
            VMEM((64, 3, 128, 128), F32),
            VMEM((3, 128, 192), BF16),
            VMEM((64, 128, 128), F32),
            SMEM((84,), jnp.int32),
            SMEM((2, 16, 128), F32),
            VMEM((128, 128), F32),
            VMEM((4, 8, 8, 128), F32),
            VMEM((2688, 256), BF16),
            VMEM((2, 8, 8, 2688), F32),
            VMEM((32, 128), F32),
            pltpu.SemaphoreType.DMA((2,)),
        ],
        compiler_params=pltpu.CompilerParams(vmem_limit_bytes=30 * 1024 * 1024),
        name="final",
    )(counts, flags, pos, charges, zup, zdn, zlo, zhi, before, inner, outer, down_inv)


def exchange(up, down, dimension):
    return (
        lax.ppermute(up, AXES, shifted(dimension, 1)),
        lax.ppermute(down, AXES, shifted(dimension, -1)),
    )


def per_device(positions, charges, counts, up_inverse, down_inverse, inner_surface, outer_surface):
    device = (lax.axis_index("gx") * 4 + lax.axis_index("gy")) * 16 + lax.axis_index("gz")
    sides = []
    for d in range(3):
        at = jnp.zeros((), jnp.int32)
        for k, b in enumerate(BITS[d]):
            at = at + jnp.left_shift(jnp.bitwise_and(jnp.right_shift(device, b), 1), k)
        sides += [at > 0, at < EXTENT[d] - 1]
    flags = jnp.stack(sides).astype(jnp.int32)
    positions = jnp.transpose(positions, (1, 0, 2))
    own, xup, xdn = upward(counts, positions, charges, outer_surface, up_inverse)
    xlo, xhi = exchange(xup, xdn, 0)
    near = near_xy((1, 2), counts, positions, charges)
    yup, ydn = pack_y(counts, positions, charges, own, xlo, xhi, near)
    ylo, yhi = exchange(yup, ydn, 1)
    near = near_xy((0, 3), counts, positions, charges, (flags, xlo, xhi, near))
    zup, zdn = pack_z(counts, positions, charges, own, xlo, xhi, yup, ylo, yhi, near)
    zlo, zhi = exchange(zup, zdn, 2)
    near = near_y(counts, flags, positions, ylo, yhi, near)
    return final(
        counts, flags, positions, charges, zup, zdn, zlo, zhi, near, inner_surface, outer_surface, down_inverse
    )


def solution(mesh):
    split = AXES
    return jax.shard_map(
        per_device,
        mesh=mesh,
        in_specs=(P(split, None, None), P(split, None), P(split), P(), P(), P(), P()),
        out_specs=P(split, None),
        check_vma=False,
    )
```

```python
import jax
import jax.numpy as jnp
from jax import lax
from jax.experimental import pallas as pl
from jax.experimental.pallas import tpu as pltpu
from jax.sharding import PartitionSpec as P

SOFTEN = 0.0025
HIGH = lax.Precision.HIGHEST
AXES = ("gx", "gy", "gz")
BITS = ((0, 3, 6), (1, 4, 7), (2, 5))
EXTENT = (8, 8, 4)
F32 = jnp.float32
BF16 = jnp.bfloat16
VMEM = pltpu.VMEM
SMEM = pltpu.SMEM
X_ROWS = 88
Y_ROWS = 136
Z_ROWS = 224


def place(q):
    return [sum(((q >> b) & 1) << k for k, b in enumerate(BITS[d])) for d in range(3)]


def linear(c):
    return sum(((c[d] >> k) & 1) << b for d in range(3) for k, b in enumerate(BITS[d]))


def shifted(dimension, step):
    pairs = []
    for q in range(256):
        c = place(q)
        c[dimension] = (c[dimension] + step) % EXTENT[dimension]
        pairs.append((q, linear(c)))
    return pairs


def lanes(shape):
    return lax.broadcasted_iota(jnp.int32, shape, len(shape) - 1)


def point_rows(pos, n):
    return jnp.concatenate([pos[d, pl.ds(n, 1), :] for d in range(3)], axis=0)


def dot(a, b):
    return jnp.dot(a, b, precision=HIGH, preferred_element_type=F32)


def upward_kernel(counts, pos, charges, outer, up_inv, own, xup, xdn, outer_b, source, density):
    oc = jnp.transpose(jnp.concatenate([outer[...], jnp.zeros((5, 64), F32)], axis=0))
    for d in range(3):
        outer_b[d] = jnp.broadcast_to(oc[:, d : d + 1], (64, 128))
    lane = lanes((1, 128))

    lane8 = lanes((64, 128))
    ones = jnp.ones((384, 128), BF16)

    def step(k, check):
        at = [8 * k + u for u in range(8)]
        loaded = [(point_rows(pos, n), charges[pl.ds(n, 1), :], counts[n]) for n in at]
        charge_rows, values = [], []
        for p, charge, count in loaded:
            q = jnp.where(lane < count, charge, 0.0)
            square = SOFTEN
            for d in range(3):
                spread = outer_b[d] - p[d : d + 1]
                square = square + spread * spread
            charge_rows.append(q)
            values.append(lax.rsqrt(square) * q)
        rest = jnp.concatenate(values[:4], axis=0)
        parts = []
        for _ in range(3):
            part = rest.astype(BF16)
            parts.append(part)
            rest = rest - part.astype(F32)
        column = jnp.dot(jnp.concatenate(parts, axis=1), ones, preferred_element_type=F32)
        columns = [column[64 * u : 64 * (u + 1)] for u in range(4)]
        columns += [jnp.sum(value, axis=1, keepdims=True) for value in values[4:]]
        for n, column in zip(at, columns):
            check = jnp.where(lane8 == n, column, check)
        for n, q in zip(at, charge_rows):
            source[pl.ds(n, 1), :] = q
        return check

    check = lax.fori_loop(0, 8, step, jnp.zeros((64, 128), F32))
    dens = jnp.transpose(dot(up_inv[...], check))[:64]
    density[...] = jnp.concatenate([dens, dens], axis=1)
    for hz in range(2):
        even = density[pl.ds(2 * hz, 16, stride=4), :]
        odd = density[pl.ds(2 * hz + 1, 16, stride=4), :]
        own[pl.ds(16 * hz, 16), :] = jnp.where(lane < 64, even, odd)
    for msg, x, xl in ((xup, 3, 2), (xdn, 0, 0)):
        for hz in range(2):
            msg[pl.ds(8 * hz, 8), :] = own[pl.ds(16 * hz + 4 * xl, 8), :]
        row = jnp.zeros((1, 128), F32)
        for k in range(16):
            n = 16 * x + k
            msg[pl.ds(16 + 4 * k, 3), :] = point_rows(pos, n)
            msg[pl.ds(16 + 4 * k + 3, 1), :] = source[pl.ds(n, 1), :]
            row = jnp.where(lane == k, counts[n].astype(F32), row)
        msg[pl.ds(80, 8), :] = jnp.broadcast_to(row, (8, 128))


def upward(counts, pos, charges, outer, up_inv):
    return pl.pallas_call(
        upward_kernel,
        out_shape=(
            jax.ShapeDtypeStruct((32, 128), F32),
            jax.ShapeDtypeStruct((X_ROWS, 128), F32),
            jax.ShapeDtypeStruct((X_ROWS, 128), F32),
        ),
        in_specs=[pl.BlockSpec(memory_space=SMEM)] + [pl.BlockSpec(memory_space=VMEM)] * 4,
        scratch_shapes=[VMEM((3, 64, 128), F32), VMEM((64, 128), F32), VMEM((64, 128), F32)],
        name="upward",
    )(counts, pos, charges, outer, up_inv)


def own_points(msg, at, pos, charges, counts, n):
    msg[pl.ds(at, 3), :] = point_rows(pos, n)
    msg[pl.ds(at + 3, 1), :] = jnp.where(lanes((1, 128)) < counts[n], charges[pl.ds(n, 1), :], 0.0)


def pack_y_kernel(counts, pos, charges, own, xlo, xhi, near, yup, ydn):
    lane = lanes((1, 128))
    row = jnp.zeros((1, 128), F32)
    for k in range(64):
        row = jnp.where(lane == k, counts[k].astype(F32), row)
    for msg, y, yl in ((yup, 3, 2), (ydn, 0, 0)):
        for hz in range(2):
            for ex in range(8):
                at = pl.ds((hz * 8 + ex) * 2, 2)
                if ex < 2:
                    msg[at, :] = xlo[pl.ds((hz * 2 + ex) * 4 + yl, 2), :]
                elif ex < 6:
                    msg[at, :] = own[pl.ds((hz * 4 + ex - 2) * 4 + yl, 2), :]
                else:
                    msg[at, :] = xhi[pl.ds((hz * 2 + ex - 6) * 4 + yl, 2), :]
        for z in range(4):
            msg[pl.ds(32 + 4 * z, 4), :] = xlo[pl.ds(16 + 4 * (4 * y + z), 4), :]
            for x in range(4):
                own_points(msg, 32 + 4 * (4 * (x + 1) + z), pos, charges, counts, 16 * x + 4 * y + z)
            msg[pl.ds(32 + 4 * (20 + z), 4), :] = xhi[pl.ds(16 + 4 * (4 * y + z), 4), :]
        msg[pl.ds(128, 1), :] = row
        msg[pl.ds(129, 1), :] = xlo[pl.ds(80, 1), :]
        msg[pl.ds(130, 1), :] = xhi[pl.ds(80, 1), :]
        msg[pl.ds(131, 5), :] = jnp.zeros((5, 128), F32)


def pack_y(counts, pos, charges, own, xlo, xhi, near):
    return pl.pallas_call(
        pack_y_kernel,
        out_shape=(jax.ShapeDtypeStruct((Y_ROWS, 128), F32),) * 2,
        in_specs=[pl.BlockSpec(memory_space=SMEM)] + [pl.BlockSpec(memory_space=VMEM)] * 5 + [pl.BlockSpec(memory_space=pl.ANY)],
        compiler_params=pltpu.CompilerParams(vmem_limit_bytes=6 * 1024 * 1024),
        name="pack_y",
    )(counts, pos, charges, own, xlo, xhi, near)


def pack_z_kernel(counts, pos, charges, own, xlo, xhi, yup, ylo, yhi, near, zup, zdn):
    for msg, z, hz in ((zup, 3, 1), (zdn, 0, 0)):
        for ex in range(8):
            at = ex * 8
            msg[pl.ds(at, 2), :] = ylo[pl.ds((hz * 8 + ex) * 2, 2), :]
            if ex < 2:
                msg[pl.ds(at + 2, 4), :] = xlo[pl.ds((hz * 2 + ex) * 4, 4), :]
            elif ex < 6:
                msg[pl.ds(at + 2, 4), :] = own[pl.ds((hz * 4 + ex - 2) * 4, 4), :]
            else:
                msg[pl.ds(at + 2, 4), :] = xhi[pl.ds((hz * 2 + ex - 6) * 4, 4), :]
            msg[pl.ds(at + 6, 2), :] = yhi[pl.ds((hz * 8 + ex) * 2, 2), :]
        for ex in range(6):
            for ey in range(6):
                at = 64 + 4 * (6 * ex + ey)
                if ey == 0:
                    msg[pl.ds(at, 4), :] = ylo[pl.ds(32 + 4 * (4 * ex + z), 4), :]
                elif ey == 5:
                    msg[pl.ds(at, 4), :] = yhi[pl.ds(32 + 4 * (4 * ex + z), 4), :]
                elif ex == 0:
                    msg[pl.ds(at, 4), :] = xlo[pl.ds(16 + 4 * (4 * (ey - 1) + z), 4), :]
                elif ex == 5:
                    msg[pl.ds(at, 4), :] = xhi[pl.ds(16 + 4 * (4 * (ey - 1) + z), 4), :]
                else:
                    own_points(msg, at, pos, charges, counts, 16 * (ex - 1) + 4 * (ey - 1) + z)
        msg[pl.ds(208, 3), :] = yup[pl.ds(128, 3), :]
        msg[pl.ds(211, 3), :] = ylo[pl.ds(128, 3), :]
        msg[pl.ds(214, 3), :] = yhi[pl.ds(128, 3), :]
        msg[pl.ds(217, 7), :] = jnp.zeros((7, 128), F32)


def pack_z(counts, pos, charges, own, xlo, xhi, yup, ylo, yhi, near):
    return pl.pallas_call(
        pack_z_kernel,
        out_shape=(jax.ShapeDtypeStruct((Z_ROWS, 128), F32),) * 2,
        in_specs=[pl.BlockSpec(memory_space=SMEM)] + [pl.BlockSpec(memory_space=VMEM)] * 8 + [pl.BlockSpec(memory_space=pl.ANY)],
        compiler_params=pltpu.CompilerParams(vmem_limit_bytes=6 * 1024 * 1024),
        name="pack_z",
    )(counts, pos, charges, own, xlo, xhi, yup, ylo, yhi, near)


def add_source(packed, base, place_at, leaf, count, cell, lane):
    off = jnp.bitwise_and(place_at, 127)
    tile = base + jnp.right_shift(place_at, 7)
    row = lax.broadcasted_iota(jnp.int32, (4, 128), 0)
    shift = jnp.where(row == 0, cell[0], jnp.where(row == 1, cell[1], jnp.where(row == 2, cell[2], 0.0)))
    rolled = pltpu.roll(leaf + shift, off, 1)
    packed[tile, pl.ds(0, 4), :] = jnp.where(lane >= off, rolled, packed[tile, pl.ds(0, 4), :])
    packed[tile + 1, pl.ds(0, 4), :] = rolled
    return place_at + count


def close_list(packed, base, end):
    packed[base + jnp.right_shift(end, 7) + 1, pl.ds(0, 4), :] = jnp.zeros((4, 128), F32)
    packed[base + jnp.right_shift(end, 7) + 2, pl.ds(0, 4), :] = jnp.zeros((4, 128), F32)


def cell_of(n):
    return jnp.right_shift(n, 4), jnp.bitwise_and(jnp.right_shift(n, 2), 3), jnp.bitwise_and(n, 3)


def spread_targets(pos, spread, turned, leaf_of, leaves):
    number = lax.broadcasted_iota(jnp.int32, (64, 128), 0)
    for d, part in enumerate(cell_of(number)):
        flat = pos[d] + part.astype(F32)
        rest = jnp.transpose(jnp.concatenate([flat, flat], axis=0))[:, :64]
        for p in range(3):
            piece = rest.astype(BF16)
            turned[pl.ds(128 * d, 128), pl.ds(64 * p, 64)] = piece
            rest = rest - piece.astype(F32)
    place_of = jnp.bitwise_and(lax.broadcasted_iota(jnp.int32, (192, 128), 0), 63)

    def step(k, carry):
        pick = jnp.concatenate(
            [jnp.where(place_of == leaf_of(4 * k + u), 1.0, 0.0).astype(BF16) for u in range(4)], axis=1
        )
        wide = jnp.dot(turned[...], pick, preferred_element_type=F32)
        for u in range(4):
            for d in range(3):
                spread[4 * k + u, d] = wide[128 * d : 128 * (d + 1), 128 * u : 128 * (u + 1)]
        return carry

    lax.fori_loop(0, leaves // 4, step, 0)


TOGETHER = ((1, 4), (2, 2), (3, 2), (4, 1))


def near_sums(i, count, spread, sums, packed, segments, fresh=True):
    lane = lanes((1, 128))
    shifts, starts, stops, upto = [], [], [], []
    have = jnp.int32(0)
    for base, start, stop in segments:
        first = jnp.right_shift(start, 7)
        number = jnp.where(stop > start, jnp.right_shift(stop + 127, 7) - first, 0)
        shifts.append(base + first - have)
        starts.append(base * 128 + start)
        stops.append(base * 128 + stop)
        have = have + number
        upto.append(have)

    def pick(values, tests):
        value = values[-1]
        for k in range(len(values) - 2, -1, -1):
            value = jnp.where(tests[k], values[k], value)
        return value

    def run(groups, together):
        rows = pl.ds(0, 8 * groups)
        blocks = lax.div(have + together - 1, together)

        def where_is(b):
            found = []
            for u in range(together):
                j = b * together + u
                inside = jnp.minimum(j, have - 1)
                tests = [inside < end for end in upto[:-1]]
                tile = jnp.maximum(pick(shifts, tests) + inside, 0)
                stop = jnp.where(j < have, pick(stops, tests), 0)
                found.append((tile, pick(starts, tests) - tile * 128, stop - tile * 128))
            return found

        def ahead(found):
            squares, charges = [], []
            for tile, low, high in found:
                keep = (lane >= low) & (lane < high)
                charges.append(jnp.where(keep, packed[tile, pl.ds(3, 1), :], 0.0))
                square = SOFTEN
                for d in range(3):
                    gap = spread[i, d, rows, :] - packed[tile, pl.ds(d, 1), :]
                    square = square + gap * gap
                squares.append(square)
            return squares, charges

        def add(acc, squares, charges):
            roots = [lax.rsqrt(square) for square in squares]
            for root, charge in zip(roots, charges):
                acc = acc + root * charge
            return acc

        def step(b, carry):
            acc, squares, charges, found = carry
            acc = add(acc, squares, charges)
            return (acc, *ahead(found), where_is(b + 1))

        begin = jnp.zeros((8 * groups, 128), F32) if fresh else sums[i, rows, :]
        acc, squares, charges, _ = lax.fori_loop(1, blocks, step, (begin, *ahead(where_is(0)), where_is(1)))
        sums[i, rows, :] = add(acc, squares, charges)

    size = jnp.right_shift(count + 31, 5)
    for k, together in TOGETHER:

        @pl.when(size == k)
        def _():
            run(4 * k, together)


def gather_sums(sums, total, leaf_of, leaves):
    wide = lanes((128, 128))
    ones = jnp.ones((256, 128), BF16)

    def step(k, carry):
        value = jnp.concatenate([sums[8 * k + u] for u in range(4)], axis=0)
        first = value.astype(BF16)
        second = (value - first.astype(F32)).astype(BF16)
        column = jnp.dot(jnp.concatenate([first, second], axis=1), ones, preferred_element_type=F32)
        columns = [column[128 * u : 128 * (u + 1)] for u in range(4)]
        columns += [jnp.sum(sums[8 * k + u], axis=1, keepdims=True) for u in range(4, 8)]
        for u, column in enumerate(columns):
            carry = jnp.where(wide == leaf_of(8 * k + u), carry + column, carry)
        return carry

    total[...] = lax.fori_loop(0, leaves // 8, step, total[...])


def near_xy_kernel(windows, *refs):
    if len(refs) == 10:
        counts, pos, charges, total, packed, spread, turned, sums, ends, _ = refs
        xlo = xhi = None
    else:
        counts, flags, pos, charges, xlo, xhi, before, total, packed, spread, turned, sums, ends, lo_counts, hi_counts, sem = refs
        a = pltpu.make_async_copy(xlo.at[pl.ds(80, 1), :], lo_counts, sem.at[0])
        b = pltpu.make_async_copy(xhi.at[pl.ds(80, 1), :], hi_counts, sem.at[1])
        a.start()
        b.start()
        a.wait()
        b.wait()
    lane4 = lanes((4, 128))
    lane = lanes((1, 128))
    total[...] = jnp.zeros((128, 128), F32) if xlo is None else before[...]
    for w, x in enumerate(windows):
        for z in range(4):
            base = (w * 4 + z) * 16
            end = jnp.int32(0)
            ends[(w * 4 + z) * 5] = end
            for y in range(4):
                for dx in (-1, 0, 1):
                    sx = x + dx
                    k = 4 * y + z
                    cell = (float(sx), float(y), float(z))
                    if 0 <= sx < 4:
                        n = 16 * sx + k
                        count = counts[n]
                        q = jnp.where(lane < count, charges[pl.ds(n, 1), :], 0.0)
                        leaf = jnp.concatenate([point_rows(pos, n), q], axis=0)
                    else:
                        msg, cnt, flag = (xlo, lo_counts, 0) if sx < 0 else (xhi, hi_counts, 1)
                        count = cnt[0, k].astype(jnp.int32) * flags[flag]
                        leaf = msg[pl.ds(16 + 4 * k, 4), :]
                    end = add_source(packed, base, end, leaf, count, cell, lane4)
                ends[(w * 4 + z) * 5 + y + 1] = end
            close_list(packed, base, end)

    def leaf_of(i):
        return jnp.bitwise_and(i, 15) + 16 * (windows[0] + jnp.right_shift(i, 4) * (windows[1] - windows[0]))

    spread_targets(pos, spread, turned, leaf_of, 32)

    def leaf_step(i, carry):
        w = jnp.right_shift(i, 4)
        n = leaf_of(i)
        x, y, z = cell_of(n)
        segments = []
        for dz in (-1, 0, 1):
            zz = jnp.clip(z + dz, 0, 3)
            lst = w * 4 + zz
            start = ends[lst * 5 + jnp.maximum(y - 1, 0)]
            stop = ends[lst * 5 + jnp.minimum(y + 1, 3) + 1]
            if dz:
                stop = jnp.where(zz == z + dz, stop, start)
            segments.append((lst * 16, start, stop))
        near_sums(i, counts[n], spread, sums, packed, segments)
        return carry

    lax.fori_loop(0, 32, leaf_step, 0)
    gather_sums(sums, total, leaf_of, 32)


def near_xy(windows, counts, pos, charges, halo=None):
    call_args = [counts, pos, charges]
    specs = [pl.BlockSpec(memory_space=SMEM)] + [pl.BlockSpec(memory_space=VMEM)] * 2
    if halo is not None:
        flags, xlo, xhi, before = halo
        call_args = [counts, flags, pos, charges, xlo, xhi, before]
        specs = [pl.BlockSpec(memory_space=SMEM)] * 2 + [pl.BlockSpec(memory_space=VMEM)] * 5
    scratch = [
        VMEM((8 * 16, 8, 128), F32),
        VMEM((32, 3, 128, 128), F32),
            VMEM((384, 192), BF16),
        VMEM((32, 128, 128), F32),
        SMEM((40,), jnp.int32),
        SMEM((1, 128), F32),
    ]
    if halo is not None:
        scratch += [SMEM((1, 128), F32), pltpu.SemaphoreType.DMA((2,))]

    def body(*refs):
        near_xy_kernel(windows, *refs)

    return pl.pallas_call(
        body,
        out_shape=jax.ShapeDtypeStruct((128, 128), F32),
        in_specs=specs,
        scratch_shapes=scratch,
        compiler_params=pltpu.CompilerParams(vmem_limit_bytes=14 * 1024 * 1024),
        cost_estimate=pl.CostEstimate(flops=150_000_000, bytes_accessed=300_000, transcendentals=10_000_000),
        name="near_x",
    )(*call_args)


def near_y_kernel(counts, flags, pos, ylo, yhi, before, total, packed, spread, turned, sums, ends, row_counts, sem):
    copies = [
        pltpu.make_async_copy(msg.at[pl.ds(128, 8), :], row_counts.at[i], sem.at[i])
        for i, msg in enumerate((ylo, yhi))
    ]
    for c in copies:
        c.start()
    for c in copies:
        c.wait()
    lane4 = lanes((4, 128))
    total[...] = before[...]
    for side, msg in enumerate((ylo, yhi)):
        sy = -1 if side == 0 else 4
        far_y = 3 if side == 0 else 0
        for z in range(4):
            lst = side * 4 + z
            end = jnp.int32(0)
            ends[lst * 7] = end
            for ex in range(6):
                if ex == 0:
                    count = row_counts[side, 1, 4 * far_y + z].astype(jnp.int32) * flags[0]
                elif ex == 5:
                    count = row_counts[side, 2, 4 * far_y + z].astype(jnp.int32) * flags[1]
                else:
                    count = row_counts[side, 0, 16 * (ex - 1) + 4 * far_y + z].astype(jnp.int32)
                count = count * flags[2 + side]
                leaf = msg[pl.ds(32 + 4 * (4 * ex + z), 4), :]
                end = add_source(packed, lst * 10, end, leaf, count, (float(ex - 1), float(sy), float(z)), lane4)
                ends[lst * 7 + ex + 1] = end
            close_list(packed, lst * 10, end)

    def leaf_of(i):
        side = jnp.right_shift(i, 4)
        x = jnp.bitwise_and(jnp.right_shift(i, 2), 3)
        return 16 * x + 12 * side + jnp.bitwise_and(i, 3)

    spread_targets(pos, spread, turned, leaf_of, 32)

    def leaf_step(i, carry):
        side = jnp.right_shift(i, 4)
        n = leaf_of(i)
        x, y, z = cell_of(n)
        segments = []
        for dz in (-1, 0, 1):
            zz = jnp.clip(z + dz, 0, 3)
            lst = side * 4 + zz
            start = ends[lst * 7 + x]
            stop = ends[lst * 7 + x + 3]
            if dz:
                stop = jnp.where(zz == z + dz, stop, start)
            segments.append((lst * 10, start, stop))
        near_sums(i, counts[n], spread, sums, packed, segments)
        return carry

    lax.fori_loop(0, 32, leaf_step, 0)
    gather_sums(sums, total, leaf_of, 32)


def near_y(counts, flags, pos, ylo, yhi, before):
    return pl.pallas_call(
        near_y_kernel,
        out_shape=jax.ShapeDtypeStruct((128, 128), F32),
        in_specs=[pl.BlockSpec(memory_space=SMEM)] * 2 + [pl.BlockSpec(memory_space=VMEM)] * 4,
        scratch_shapes=[
            VMEM((8 * 10, 8, 128), F32),
            VMEM((32, 3, 128, 128), F32),
            VMEM((384, 192), BF16),
            VMEM((32, 128, 128), F32),
            SMEM((56,), jnp.int32),
            SMEM((2, 8, 128), F32),
            pltpu.SemaphoreType.DMA((2,)),
        ],
        compiler_params=pltpu.CompilerParams(vmem_limit_bytes=14 * 1024 * 1024),
        cost_estimate=pl.CostEstimate(flops=60_000_000, bytes_accessed=300_000, transcendentals=4_000_000),
        name="near_y",
    )(counts, flags, pos, ylo, yhi, before)


def final_kernel(
    counts, flags, pos, charges, zup, zdn, zlo, zhi, before, inner, outer, down_inv,
    out, packed, spread, turned, sums, ends, row_counts, total, grid, weights, left, local, sem,
):
    copies = [
        pltpu.make_async_copy(msg.at[pl.ds(208, 16), :], row_counts.at[i], sem.at[i])
        for i, msg in enumerate((zlo, zhi))
    ]
    for c in copies:
        c.start()
    grid[1] = zdn[pl.ds(0, 64), :].reshape(8, 8, 128)
    grid[2] = zup[pl.ds(0, 64), :].reshape(8, 8, 128)
    grid[0] = zlo[pl.ds(0, 64), :].reshape(8, 8, 128)
    grid[3] = zhi[pl.ds(0, 64), :].reshape(8, 8, 128)

    @pl.when(flags[0] == 0)
    def _():
        grid[:, pl.ds(0, 2)] = jnp.zeros((4, 2, 8, 128), F32)

    @pl.when(flags[1] == 0)
    def _():
        grid[:, pl.ds(6, 2)] = jnp.zeros((4, 2, 8, 128), F32)

    @pl.when(flags[2] == 0)
    def _():
        grid[:, :, pl.ds(0, 2), :] = jnp.zeros((4, 8, 2, 128), F32)

    @pl.when(flags[3] == 0)
    def _():
        grid[:, :, pl.ds(6, 2), :] = jnp.zeros((4, 8, 2, 128), F32)

    @pl.when(flags[4] == 0)
    def _():
        grid[0] = jnp.zeros((8, 8, 128), F32)

    @pl.when(flags[5] == 0)
    def _():
        grid[3] = jnp.zeros((8, 8, 128), F32)

    odd_row = jnp.bitwise_and(lax.broadcasted_iota(jnp.int32, (8, 128), 0), 1) == 1
    for oy in range(7):
        for x in range(8):
            for hb in range(3):
                begin = min(max(oy - 1, 0), 4)
                both = jnp.concatenate(
                    [grid[hb, x, pl.ds(begin, 4), :], grid[hb + 1, x, pl.ds(begin, 4), :]], axis=0
                )
                if oy == 0:
                    both = jnp.where(odd_row, pltpu.roll(both, 1, 0), 0.0)
                elif oy == 6:
                    both = jnp.where(odd_row, 0.0, pltpu.roll(both, 7, 0))
                first = both.astype(BF16)
                left[0, x, :, pl.ds(oy * 384 + hb * 128, 128)] = first.astype(F32)
                left[1, x, :, pl.ds(oy * 384 + hb * 128, 128)] = both - first.astype(F32)

    inner_rows = jnp.concatenate([inner[...], jnp.zeros((5, 64), F32)], axis=0)
    inner_cols = jnp.transpose(inner_rows)
    diff = [
        jnp.concatenate([inner[d : d + 1, :], inner[d : d + 1, :]], axis=1) - jnp.broadcast_to(inner_cols[:, d : d + 1], (64, 128))
        for d in range(3)
    ]
    wide = lanes((64, 128))
    right = jnp.where(wide >= 64, 1.0, 0.0)
    zsq = []
    for sz in range(6):
        offset = float(sz - 2) - right
        gap = diff[2] - offset
        zsq.append(gap * gap + SOFTEN)
    check = [None] * 4

    def over_x(ox, xs, rows):
        gap_x = diff[0] - float(ox)
        xsq = gap_x * gap_x
        for oy in range(-3, 4):
            gap_y = diff[1] - float(oy)
            xysq = xsq + gap_y * gap_y
            for sz in range(6):
                value = lax.rsqrt(xysq + zsq[sz])
                if max(abs(ox), abs(oy)) < 2:
                    left_near = abs(sz - 2) < 2
                    right_near = abs(sz - 3) < 2
                    if left_near:
                        value = jnp.where(wide < 64, 0.0, value)
                    if right_near:
                        value = jnp.where(wide >= 64, 0.0, value)
                first = value.astype(BF16)
                at = pl.ds((oy + 3) * 384 + sz * 64, 64)
                weights[at, pl.ds(0, 128)] = first
                weights[at, pl.ds(128, 128)] = (value - first.astype(F32)).astype(BF16)
        m = 8 * len(xs)
        lhs = jnp.concatenate([left[p, x] for p in range(2) for x in rows], axis=0).astype(BF16)
        prod = jnp.dot(lhs, weights[...], preferred_element_type=F32)
        part = prod[:m, :128] + prod[:m, 128:] + prod[m:, :128]
        for i, x in enumerate(xs):
            piece = part[8 * i : 8 * i + 8]
            check[x] = piece if check[x] is None else check[x] + piece

    for ox in range(-3, 4):
        if ox == -3:
            xs = (1, 3)
        elif ox == 3:
            xs = (0, 2)
        else:
            xs = (0, 1, 2, 3)
        over_x(ox, xs, [x + ox + 2 for x in xs])
    down = check_to_local(jnp.concatenate(check, axis=0), down_inv)
    local[...] = down

    for c in copies:
        c.wait()
    lane4 = lanes((4, 128))
    total[...] = before[...]
    for side, msg in enumerate((zlo, zhi)):
        sz = -1 if side == 0 else 4
        far_z = 3 if side == 0 else 0
        for ey in range(6):
            lst = side * 6 + ey
            end = jnp.int32(0)
            ends[lst * 7] = end
            for ex in range(6):
                group = 3 if ey == 0 else (6 if ey == 5 else 0)
                y = 3 if ey == 0 else (0 if ey == 5 else ey - 1)
                if ex == 0:
                    count = row_counts[side, group + 1, 4 * y + far_z].astype(jnp.int32) * flags[0]
                elif ex == 5:
                    count = row_counts[side, group + 2, 4 * y + far_z].astype(jnp.int32) * flags[1]
                else:
                    count = row_counts[side, group, 16 * (ex - 1) + 4 * y + far_z].astype(jnp.int32)
                if ey == 0:
                    count = count * flags[2]
                elif ey == 5:
                    count = count * flags[3]
                count = count * flags[4 + side]
                leaf = msg[pl.ds(64 + 4 * (6 * ex + ey), 4), :]
                end = add_source(packed, lst * 10, end, leaf, count, (float(ex - 1), float(ey - 1), float(sz)), lane4)
                ends[lst * 7 + ex + 1] = end
            close_list(packed, lst * 10, end)

    outer_twice = jnp.concatenate([outer[...], outer[...]], axis=1)
    lane = lanes((1, 128))

    spread_targets(pos, spread, turned, lambda i: i, 64)

    def far_step(n, carry):
        cell = cell_of(n)
        x, y, z = cell
        weight = local[pl.ds(x * 8 + jnp.right_shift(z, 1) * 4 + y, 1), :]
        weight = jnp.where(jnp.right_shift(lane, 6) == jnp.bitwise_and(z, 1), weight, 0.0)
        square = SOFTEN
        for d in range(3):
            gap = spread[n, d] - (outer_twice[d : d + 1] + cell[d].astype(F32))
            square = square + gap * gap
        sums[n] = lax.rsqrt(square) * weight
        return carry

    lax.fori_loop(0, 64, far_step, 0, unroll=2)

    def leaf_step(i, carry):
        side = jnp.bitwise_and(i, 1)
        n = jnp.right_shift(i, 1) * 4 + 3 * side
        x, y, z = cell_of(n)
        segments = []
        for dy in range(3):
            lst = side * 6 + y + dy
            segments.append((lst * 10, ends[lst * 7 + x], ends[lst * 7 + x + 3]))
        near_sums(n, counts[n], spread, sums, packed, segments, fresh=False)
        return carry

    lax.fori_loop(0, 32, leaf_step, 0)
    gather_sums(sums, total, lambda i: i, 64)
    row = lax.broadcasted_iota(jnp.int32, (64, 1), 0)
    full = jnp.zeros((64, 1), jnp.int32)
    for n in range(64):
        full = jnp.where(row == n, counts[n], full)
    live = lanes((64, 128)) < full
    own_term = lax.rsqrt(jnp.full((64, 128), SOFTEN, F32))
    out[...] = jnp.where(live, jnp.transpose(total[...])[:64] - own_term * charges[...], 0.0)


def check_to_local(check, down_inv):
    flat = jnp.transpose(down_inv[...])
    zero = jnp.zeros((64, 64), F32)
    block = jnp.concatenate(
        [jnp.concatenate([flat, zero], axis=1), jnp.concatenate([zero, flat], axis=1)], axis=0
    )
    return dot(check, block)


def final(counts, flags, pos, charges, zup, zdn, zlo, zhi, before, inner, outer, down_inv):
    return pl.pallas_call(
        final_kernel,
        out_shape=jax.ShapeDtypeStruct((64, 128), F32),
        in_specs=[pl.BlockSpec(memory_space=SMEM)] * 2 + [pl.BlockSpec(memory_space=VMEM)] * 10,
        scratch_shapes=[
            VMEM((12 * 10, 8, 128), F32),
            VMEM((64, 3, 128, 128), F32),
            VMEM((384, 192), BF16),
            VMEM((64, 128, 128), F32),
            SMEM((84,), jnp.int32),
            SMEM((2, 16, 128), F32),
            VMEM((128, 128), F32),
            VMEM((4, 8, 8, 128), F32),
            VMEM((2688, 256), BF16),
            VMEM((2, 8, 8, 2688), F32),
            VMEM((32, 128), F32),
            pltpu.SemaphoreType.DMA((2,)),
        ],
        compiler_params=pltpu.CompilerParams(vmem_limit_bytes=30 * 1024 * 1024),
        name="final",
    )(counts, flags, pos, charges, zup, zdn, zlo, zhi, before, inner, outer, down_inv)


def exchange(up, down, dimension):
    return (
        lax.ppermute(up, AXES, shifted(dimension, 1)),
        lax.ppermute(down, AXES, shifted(dimension, -1)),
    )


def per_device(positions, charges, counts, up_inverse, down_inverse, inner_surface, outer_surface):
    device = (lax.axis_index("gx") * 4 + lax.axis_index("gy")) * 16 + lax.axis_index("gz")
    sides = []
    for d in range(3):
        at = jnp.zeros((), jnp.int32)
        for k, b in enumerate(BITS[d]):
            at = at + jnp.left_shift(jnp.bitwise_and(jnp.right_shift(device, b), 1), k)
        sides += [at > 0, at < EXTENT[d] - 1]
    flags = jnp.stack(sides).astype(jnp.int32)
    positions = jnp.transpose(positions, (1, 0, 2))
    own, xup, xdn = upward(counts, positions, charges, outer_surface, up_inverse)
    xlo, xhi = exchange(xup, xdn, 0)
    near = near_xy((1, 2), counts, positions, charges)
    yup, ydn = pack_y(counts, positions, charges, own, xlo, xhi, near)
    ylo, yhi = exchange(yup, ydn, 1)
    near = near_xy((0, 3), counts, positions, charges, (flags, xlo, xhi, near))
    zup, zdn = pack_z(counts, positions, charges, own, xlo, xhi, yup, ylo, yhi, near)
    zlo, zhi = exchange(zup, zdn, 2)
    near = near_y(counts, flags, positions, ylo, yhi, near)
    return final(
        counts, flags, positions, charges, zup, zdn, zlo, zhi, near, inner_surface, outer_surface, down_inverse
    )


def solution(mesh):
    split = AXES
    return jax.shard_map(
        per_device,
        mesh=mesh,
        in_specs=(P(split, None, None), P(split, None), P(split), P(), P(), P(), P()),
        out_specs=P(split, None),
        check_vma=False,
    )
```

```python
import jax
import jax.numpy as jnp
from jax import lax
from jax.experimental import pallas as pl
from jax.experimental.pallas import tpu as pltpu
from jax.sharding import PartitionSpec as P

SOFTEN = 0.0025
HIGH = lax.Precision.HIGHEST
AXES = ("gx", "gy", "gz")
BITS = ((0, 3, 6), (1, 4, 7), (2, 5))
EXTENT = (8, 8, 4)
F32 = jnp.float32
BF16 = jnp.bfloat16
VMEM = pltpu.VMEM
SMEM = pltpu.SMEM
X_ROWS = 88
Y_ROWS = 136
Z_ROWS = 224


def place(q):
    return [sum(((q >> b) & 1) << k for k, b in enumerate(BITS[d])) for d in range(3)]


def linear(c):
    return sum(((c[d] >> k) & 1) << b for d in range(3) for k, b in enumerate(BITS[d]))


def shifted(dimension, step):
    pairs = []
    for q in range(256):
        c = place(q)
        c[dimension] = (c[dimension] + step) % EXTENT[dimension]
        pairs.append((q, linear(c)))
    return pairs


def lanes(shape):
    return lax.broadcasted_iota(jnp.int32, shape, len(shape) - 1)


def point_rows(pos, n):
    return jnp.concatenate([pos[d, pl.ds(n, 1), :] for d in range(3)], axis=0)


def dot(a, b):
    return jnp.dot(a, b, precision=HIGH, preferred_element_type=F32)


def upward_kernel(counts, pos, charges, outer, up_inv, own, xup, xdn, outer_b, source, density):
    oc = jnp.transpose(jnp.concatenate([outer[...], jnp.zeros((5, 64), F32)], axis=0))
    for d in range(3):
        outer_b[d] = jnp.broadcast_to(oc[:, d : d + 1], (64, 128))
    lane = lanes((1, 128))

    lane8 = lanes((64, 128))
    ones = jnp.ones((384, 128), BF16)

    def step(k, check):
        at = [8 * k + u for u in range(8)]
        loaded = [(point_rows(pos, n), charges[pl.ds(n, 1), :], counts[n]) for n in at]
        charge_rows, values = [], []
        for p, charge, count in loaded:
            q = jnp.where(lane < count, charge, 0.0)
            square = SOFTEN
            for d in range(3):
                spread = outer_b[d] - p[d : d + 1]
                square = square + spread * spread
            charge_rows.append(q)
            values.append(lax.rsqrt(square) * q)
        rest = jnp.concatenate(values[:4], axis=0)
        parts = []
        for _ in range(3):
            part = rest.astype(BF16)
            parts.append(part)
            rest = rest - part.astype(F32)
        column = jnp.dot(jnp.concatenate(parts, axis=1), ones, preferred_element_type=F32)
        columns = [column[64 * u : 64 * (u + 1)] for u in range(4)]
        columns += [jnp.sum(value, axis=1, keepdims=True) for value in values[4:]]
        for n, column in zip(at, columns):
            check = jnp.where(lane8 == n, column, check)
        for n, q in zip(at, charge_rows):
            source[pl.ds(n, 1), :] = q
        return check

    check = lax.fori_loop(0, 8, step, jnp.zeros((64, 128), F32))
    dens = jnp.transpose(dot(up_inv[...], check))[:64]
    density[...] = jnp.concatenate([dens, dens], axis=1)
    for hz in range(2):
        even = density[pl.ds(2 * hz, 16, stride=4), :]
        odd = density[pl.ds(2 * hz + 1, 16, stride=4), :]
        own[pl.ds(16 * hz, 16), :] = jnp.where(lane < 64, even, odd)
    for msg, x, xl in ((xup, 3, 2), (xdn, 0, 0)):
        for hz in range(2):
            msg[pl.ds(8 * hz, 8), :] = own[pl.ds(16 * hz + 4 * xl, 8), :]
        row = jnp.zeros((1, 128), F32)
        for k in range(16):
            n = 16 * x + k
            msg[pl.ds(16 + 4 * k, 3), :] = point_rows(pos, n)
            msg[pl.ds(16 + 4 * k + 3, 1), :] = source[pl.ds(n, 1), :]
            row = jnp.where(lane == k, counts[n].astype(F32), row)
        msg[pl.ds(80, 8), :] = jnp.broadcast_to(row, (8, 128))


def upward(counts, pos, charges, outer, up_inv):
    return pl.pallas_call(
        upward_kernel,
        out_shape=(
            jax.ShapeDtypeStruct((32, 128), F32),
            jax.ShapeDtypeStruct((X_ROWS, 128), F32),
            jax.ShapeDtypeStruct((X_ROWS, 128), F32),
        ),
        in_specs=[pl.BlockSpec(memory_space=SMEM)] + [pl.BlockSpec(memory_space=VMEM)] * 4,
        scratch_shapes=[VMEM((3, 64, 128), F32), VMEM((64, 128), F32), VMEM((64, 128), F32)],
        name="upward",
    )(counts, pos, charges, outer, up_inv)


def own_points(msg, at, pos, charges, counts, n):
    msg[pl.ds(at, 3), :] = point_rows(pos, n)
    msg[pl.ds(at + 3, 1), :] = jnp.where(lanes((1, 128)) < counts[n], charges[pl.ds(n, 1), :], 0.0)


def pack_y_kernel(counts, pos, charges, own, xlo, xhi, near, yup, ydn):
    lane = lanes((1, 128))
    row = jnp.zeros((1, 128), F32)
    for k in range(64):
        row = jnp.where(lane == k, counts[k].astype(F32), row)
    for msg, y, yl in ((yup, 3, 2), (ydn, 0, 0)):
        for hz in range(2):
            for ex in range(8):
                at = pl.ds((hz * 8 + ex) * 2, 2)
                if ex < 2:
                    msg[at, :] = xlo[pl.ds((hz * 2 + ex) * 4 + yl, 2), :]
                elif ex < 6:
                    msg[at, :] = own[pl.ds((hz * 4 + ex - 2) * 4 + yl, 2), :]
                else:
                    msg[at, :] = xhi[pl.ds((hz * 2 + ex - 6) * 4 + yl, 2), :]
        for z in range(4):
            msg[pl.ds(32 + 4 * z, 4), :] = xlo[pl.ds(16 + 4 * (4 * y + z), 4), :]
            for x in range(4):
                own_points(msg, 32 + 4 * (4 * (x + 1) + z), pos, charges, counts, 16 * x + 4 * y + z)
            msg[pl.ds(32 + 4 * (20 + z), 4), :] = xhi[pl.ds(16 + 4 * (4 * y + z), 4), :]
        msg[pl.ds(128, 1), :] = row
        msg[pl.ds(129, 1), :] = xlo[pl.ds(80, 1), :]
        msg[pl.ds(130, 1), :] = xhi[pl.ds(80, 1), :]
        msg[pl.ds(131, 5), :] = jnp.zeros((5, 128), F32)


def pack_y(counts, pos, charges, own, xlo, xhi, near):
    return pl.pallas_call(
        pack_y_kernel,
        out_shape=(jax.ShapeDtypeStruct((Y_ROWS, 128), F32),) * 2,
        in_specs=[pl.BlockSpec(memory_space=SMEM)] + [pl.BlockSpec(memory_space=VMEM)] * 5 + [pl.BlockSpec(memory_space=pl.ANY)],
        compiler_params=pltpu.CompilerParams(vmem_limit_bytes=6 * 1024 * 1024),
        name="pack_y",
    )(counts, pos, charges, own, xlo, xhi, near)


def pack_z_kernel(counts, pos, charges, own, xlo, xhi, yup, ylo, yhi, near, zup, zdn):
    for msg, z, hz in ((zup, 3, 1), (zdn, 0, 0)):
        for ex in range(8):
            at = ex * 8
            msg[pl.ds(at, 2), :] = ylo[pl.ds((hz * 8 + ex) * 2, 2), :]
            if ex < 2:
                msg[pl.ds(at + 2, 4), :] = xlo[pl.ds((hz * 2 + ex) * 4, 4), :]
            elif ex < 6:
                msg[pl.ds(at + 2, 4), :] = own[pl.ds((hz * 4 + ex - 2) * 4, 4), :]
            else:
                msg[pl.ds(at + 2, 4), :] = xhi[pl.ds((hz * 2 + ex - 6) * 4, 4), :]
            msg[pl.ds(at + 6, 2), :] = yhi[pl.ds((hz * 8 + ex) * 2, 2), :]
        for ex in range(6):
            for ey in range(6):
                at = 64 + 4 * (6 * ex + ey)
                if ey == 0:
                    msg[pl.ds(at, 4), :] = ylo[pl.ds(32 + 4 * (4 * ex + z), 4), :]
                elif ey == 5:
                    msg[pl.ds(at, 4), :] = yhi[pl.ds(32 + 4 * (4 * ex + z), 4), :]
                elif ex == 0:
                    msg[pl.ds(at, 4), :] = xlo[pl.ds(16 + 4 * (4 * (ey - 1) + z), 4), :]
                elif ex == 5:
                    msg[pl.ds(at, 4), :] = xhi[pl.ds(16 + 4 * (4 * (ey - 1) + z), 4), :]
                else:
                    own_points(msg, at, pos, charges, counts, 16 * (ex - 1) + 4 * (ey - 1) + z)
        msg[pl.ds(208, 3), :] = yup[pl.ds(128, 3), :]
        msg[pl.ds(211, 3), :] = ylo[pl.ds(128, 3), :]
        msg[pl.ds(214, 3), :] = yhi[pl.ds(128, 3), :]
        msg[pl.ds(217, 7), :] = jnp.zeros((7, 128), F32)


def pack_z(counts, pos, charges, own, xlo, xhi, yup, ylo, yhi, near):
    return pl.pallas_call(
        pack_z_kernel,
        out_shape=(jax.ShapeDtypeStruct((Z_ROWS, 128), F32),) * 2,
        in_specs=[pl.BlockSpec(memory_space=SMEM)] + [pl.BlockSpec(memory_space=VMEM)] * 8 + [pl.BlockSpec(memory_space=pl.ANY)],
        compiler_params=pltpu.CompilerParams(vmem_limit_bytes=6 * 1024 * 1024),
        name="pack_z",
    )(counts, pos, charges, own, xlo, xhi, yup, ylo, yhi, near)


def add_source(packed, base, place_at, leaf, count, cell, lane):
    off = jnp.bitwise_and(place_at, 127)
    tile = base + jnp.right_shift(place_at, 7)
    row = lax.broadcasted_iota(jnp.int32, (4, 128), 0)
    shift = jnp.where(row == 0, cell[0], jnp.where(row == 1, cell[1], jnp.where(row == 2, cell[2], 0.0)))
    rolled = pltpu.roll(leaf + shift, off, 1)
    packed[tile, pl.ds(0, 4), :] = jnp.where(lane >= off, rolled, packed[tile, pl.ds(0, 4), :])
    packed[tile + 1, pl.ds(0, 4), :] = rolled
    return place_at + count


def close_list(packed, base, end):
    packed[base + jnp.right_shift(end, 7) + 1, pl.ds(0, 4), :] = jnp.zeros((4, 128), F32)
    packed[base + jnp.right_shift(end, 7) + 2, pl.ds(0, 4), :] = jnp.zeros((4, 128), F32)


def cell_of(n):
    return jnp.right_shift(n, 4), jnp.bitwise_and(jnp.right_shift(n, 2), 3), jnp.bitwise_and(n, 3)


def spread_targets(pos, spread, turned, leaf_of, leaves):
    number = lax.broadcasted_iota(jnp.int32, (64, 128), 0)
    for d, part in enumerate(cell_of(number)):
        flat = pos[d] + part.astype(F32)
        rest = jnp.transpose(jnp.concatenate([flat, flat], axis=0))[:, :64]
        for p in range(3):
            piece = rest.astype(BF16)
            turned[pl.ds(128 * d, 128), pl.ds(64 * p, 64)] = piece
            rest = rest - piece.astype(F32)
    place_of = jnp.bitwise_and(lax.broadcasted_iota(jnp.int32, (192, 128), 0), 63)

    def step(k, carry):
        pick = jnp.concatenate(
            [jnp.where(place_of == leaf_of(4 * k + u), 1.0, 0.0).astype(BF16) for u in range(4)], axis=1
        )
        wide = jnp.dot(turned[...], pick, preferred_element_type=F32)
        for u in range(4):
            for d in range(3):
                spread[4 * k + u, d] = wide[128 * d : 128 * (d + 1), 128 * u : 128 * (u + 1)]
        return carry

    lax.fori_loop(0, leaves // 4, step, 0)


TOGETHER = ((1, 4), (2, 2), (3, 2), (4, 1))


def near_sums(i, count, spread, sums, packed, segments):
    lane = lanes((1, 128))
    shifts, starts, stops, upto = [], [], [], []
    have = jnp.int32(0)
    for base, start, stop in segments:
        first = jnp.right_shift(start, 7)
        number = jnp.where(stop > start, jnp.right_shift(stop + 127, 7) - first, 0)
        shifts.append(base + first - have)
        starts.append(base * 128 + start)
        stops.append(base * 128 + stop)
        have = have + number
        upto.append(have)

    def pick(values, tests):
        value = values[-1]
        for k in range(len(values) - 2, -1, -1):
            value = jnp.where(tests[k], values[k], value)
        return value

    def run(groups, together):
        rows = pl.ds(0, 8 * groups)
        blocks = lax.div(have + together - 1, together)

        def where_is(b):
            found = []
            for u in range(together):
                j = b * together + u
                inside = jnp.maximum(jnp.minimum(j, have - 1), 0)
                tests = [inside < end for end in upto[:-1]]
                tile = pick(shifts, tests) + inside
                stop = jnp.where(j < have, pick(stops, tests), 0)
                found.append((tile, pick(starts, tests) - tile * 128, stop - tile * 128))
            return found

        def ahead(found):
            squares, charges = [], []
            for tile, low, high in found:
                keep = (lane >= low) & (lane < high)
                charges.append(jnp.where(keep, packed[tile, pl.ds(3, 1), :], 0.0))
                square = SOFTEN
                for d in range(3):
                    gap = spread[i, d, rows, :] - packed[tile, pl.ds(d, 1), :]
                    square = square + gap * gap
                squares.append(square)
            return squares, charges

        def add(acc, squares, charges):
            roots = [lax.rsqrt(square) for square in squares]
            for root, charge in zip(roots, charges):
                acc = acc + root * charge
            return acc

        def step(b, carry):
            acc, squares, charges, found = carry
            acc = add(acc, squares, charges)
            return (acc, *ahead(found), where_is(b + 1))

        begin = jnp.zeros((8 * groups, 128), F32)
        acc, squares, charges, _ = lax.fori_loop(1, blocks, step, (begin, *ahead(where_is(0)), where_is(1)))
        sums[i, rows, :] = add(acc, squares, charges)

    size = jnp.right_shift(count + 31, 5)
    for k, together in TOGETHER:

        @pl.when(size == k)
        def _():
            run(4 * k, together)


def gather_sums(sums, total, leaf_of, leaves):
    wide = lanes((128, 128))
    ones = jnp.ones((256, 128), BF16)

    def step(k, carry):
        value = jnp.concatenate([sums[8 * k + u] for u in range(4)], axis=0)
        first = value.astype(BF16)
        second = (value - first.astype(F32)).astype(BF16)
        column = jnp.dot(jnp.concatenate([first, second], axis=1), ones, preferred_element_type=F32)
        columns = [column[128 * u : 128 * (u + 1)] for u in range(4)]
        columns += [jnp.sum(sums[8 * k + u], axis=1, keepdims=True) for u in range(4, 8)]
        for u, column in enumerate(columns):
            carry = jnp.where(wide == leaf_of(8 * k + u), carry + column, carry)
        return carry

    total[...] = lax.fori_loop(0, leaves // 8, step, total[...])


def near_xy_kernel(windows, *refs):
    if len(refs) == 10:
        counts, pos, charges, total, packed, spread, turned, sums, ends, _ = refs
        xlo = xhi = None
    else:
        counts, flags, pos, charges, xlo, xhi, before, total, packed, spread, turned, sums, ends, lo_counts, hi_counts, sem = refs
        a = pltpu.make_async_copy(xlo.at[pl.ds(80, 1), :], lo_counts, sem.at[0])
        b = pltpu.make_async_copy(xhi.at[pl.ds(80, 1), :], hi_counts, sem.at[1])
        a.start()
        b.start()
        a.wait()
        b.wait()
    lane4 = lanes((4, 128))
    lane = lanes((1, 128))
    total[...] = jnp.zeros((128, 128), F32) if xlo is None else before[...]
    for w, x in enumerate(windows):
        for z in range(4):
            base = (w * 4 + z) * 16
            end = jnp.int32(0)
            ends[(w * 4 + z) * 5] = end
            for y in range(4):
                for dx in (-1, 0, 1):
                    sx = x + dx
                    k = 4 * y + z
                    cell = (float(sx), float(y), float(z))
                    if 0 <= sx < 4:
                        n = 16 * sx + k
                        count = counts[n]
                        q = jnp.where(lane < count, charges[pl.ds(n, 1), :], 0.0)
                        leaf = jnp.concatenate([point_rows(pos, n), q], axis=0)
                    else:
                        msg, cnt, flag = (xlo, lo_counts, 0) if sx < 0 else (xhi, hi_counts, 1)
                        count = cnt[0, k].astype(jnp.int32) * flags[flag]
                        leaf = msg[pl.ds(16 + 4 * k, 4), :]
                    end = add_source(packed, base, end, leaf, count, cell, lane4)
                ends[(w * 4 + z) * 5 + y + 1] = end
            close_list(packed, base, end)

    def leaf_of(i):
        return jnp.bitwise_and(i, 15) + 16 * (windows[0] + jnp.right_shift(i, 4) * (windows[1] - windows[0]))

    spread_targets(pos, spread, turned, leaf_of, 32)

    def leaf_step(i, carry):
        w = jnp.right_shift(i, 4)
        n = leaf_of(i)
        x, y, z = cell_of(n)
        segments = []
        for dz in (-1, 0, 1):
            zz = jnp.clip(z + dz, 0, 3)
            lst = w * 4 + zz
            start = ends[lst * 5 + jnp.maximum(y - 1, 0)]
            stop = ends[lst * 5 + jnp.minimum(y + 1, 3) + 1]
            if dz:
                stop = jnp.where(zz == z + dz, stop, start)
            segments.append((lst * 16, start, stop))
        near_sums(i, counts[n], spread, sums, packed, segments)
        return carry

    lax.fori_loop(0, 32, leaf_step, 0)
    gather_sums(sums, total, leaf_of, 32)


def near_xy(windows, counts, pos, charges, halo=None):
    call_args = [counts, pos, charges]
    specs = [pl.BlockSpec(memory_space=SMEM)] + [pl.BlockSpec(memory_space=VMEM)] * 2
    if halo is not None:
        flags, xlo, xhi, before = halo
        call_args = [counts, flags, pos, charges, xlo, xhi, before]
        specs = [pl.BlockSpec(memory_space=SMEM)] * 2 + [pl.BlockSpec(memory_space=VMEM)] * 5
    scratch = [
        VMEM((8 * 16, 8, 128), F32),
        VMEM((32, 3, 128, 128), F32),
            VMEM((384, 192), BF16),
        VMEM((32, 128, 128), F32),
        SMEM((40,), jnp.int32),
        SMEM((1, 128), F32),
    ]
    if halo is not None:
        scratch += [SMEM((1, 128), F32), pltpu.SemaphoreType.DMA((2,))]

    def body(*refs):
        near_xy_kernel(windows, *refs)

    return pl.pallas_call(
        body,
        out_shape=jax.ShapeDtypeStruct((128, 128), F32),
        in_specs=specs,
        scratch_shapes=scratch,
        compiler_params=pltpu.CompilerParams(vmem_limit_bytes=14 * 1024 * 1024),
        cost_estimate=pl.CostEstimate(flops=150_000_000, bytes_accessed=300_000, transcendentals=10_000_000),
        name="near_x",
    )(*call_args)


def near_y_kernel(counts, flags, pos, ylo, yhi, before, total, packed, spread, turned, sums, ends, row_counts, sem):
    copies = [
        pltpu.make_async_copy(msg.at[pl.ds(128, 8), :], row_counts.at[i], sem.at[i])
        for i, msg in enumerate((ylo, yhi))
    ]
    for c in copies:
        c.start()
    for c in copies:
        c.wait()
    lane4 = lanes((4, 128))
    total[...] = before[...]
    for side, msg in enumerate((ylo, yhi)):
        sy = -1 if side == 0 else 4
        far_y = 3 if side == 0 else 0
        for z in range(4):
            lst = side * 4 + z
            end = jnp.int32(0)
            ends[lst * 7] = end
            for ex in range(6):
                if ex == 0:
                    count = row_counts[side, 1, 4 * far_y + z].astype(jnp.int32) * flags[0]
                elif ex == 5:
                    count = row_counts[side, 2, 4 * far_y + z].astype(jnp.int32) * flags[1]
                else:
                    count = row_counts[side, 0, 16 * (ex - 1) + 4 * far_y + z].astype(jnp.int32)
                count = count * flags[2 + side]
                leaf = msg[pl.ds(32 + 4 * (4 * ex + z), 4), :]
                end = add_source(packed, lst * 10, end, leaf, count, (float(ex - 1), float(sy), float(z)), lane4)
                ends[lst * 7 + ex + 1] = end
            close_list(packed, lst * 10, end)

    def leaf_of(i):
        side = jnp.right_shift(i, 4)
        x = jnp.bitwise_and(jnp.right_shift(i, 2), 3)
        return 16 * x + 12 * side + jnp.bitwise_and(i, 3)

    spread_targets(pos, spread, turned, leaf_of, 32)

    def leaf_step(i, carry):
        side = jnp.right_shift(i, 4)
        n = leaf_of(i)
        x, y, z = cell_of(n)
        segments = []
        for dz in (-1, 0, 1):
            zz = jnp.clip(z + dz, 0, 3)
            lst = side * 4 + zz
            start = ends[lst * 7 + x]
            stop = ends[lst * 7 + x + 3]
            if dz:
                stop = jnp.where(zz == z + dz, stop, start)
            segments.append((lst * 10, start, stop))
        near_sums(i, counts[n], spread, sums, packed, segments)
        return carry

    lax.fori_loop(0, 32, leaf_step, 0)
    gather_sums(sums, total, leaf_of, 32)


def near_y(counts, flags, pos, ylo, yhi, before):
    return pl.pallas_call(
        near_y_kernel,
        out_shape=jax.ShapeDtypeStruct((128, 128), F32),
        in_specs=[pl.BlockSpec(memory_space=SMEM)] * 2 + [pl.BlockSpec(memory_space=VMEM)] * 4,
        scratch_shapes=[
            VMEM((8 * 10, 8, 128), F32),
            VMEM((32, 3, 128, 128), F32),
            VMEM((384, 192), BF16),
            VMEM((32, 128, 128), F32),
            SMEM((56,), jnp.int32),
            SMEM((2, 8, 128), F32),
            pltpu.SemaphoreType.DMA((2,)),
        ],
        compiler_params=pltpu.CompilerParams(vmem_limit_bytes=14 * 1024 * 1024),
        cost_estimate=pl.CostEstimate(flops=60_000_000, bytes_accessed=300_000, transcendentals=4_000_000),
        name="near_y",
    )(counts, flags, pos, ylo, yhi, before)


def final_kernel(
    counts, flags, pos, charges, zup, zdn, zlo, zhi, before, inner, outer, down_inv,
    out, packed, spread, turned, sums, ends, row_counts, total, grid, weights, left, local, far, outer_b, sem,
):
    copies = [
        pltpu.make_async_copy(msg.at[pl.ds(208, 16), :], row_counts.at[i], sem.at[i])
        for i, msg in enumerate((zlo, zhi))
    ]
    for c in copies:
        c.start()
    grid[1] = zdn[pl.ds(0, 64), :].reshape(8, 8, 128)
    grid[2] = zup[pl.ds(0, 64), :].reshape(8, 8, 128)
    grid[0] = zlo[pl.ds(0, 64), :].reshape(8, 8, 128)
    grid[3] = zhi[pl.ds(0, 64), :].reshape(8, 8, 128)

    @pl.when(flags[0] == 0)
    def _():
        grid[:, pl.ds(0, 2)] = jnp.zeros((4, 2, 8, 128), F32)

    @pl.when(flags[1] == 0)
    def _():
        grid[:, pl.ds(6, 2)] = jnp.zeros((4, 2, 8, 128), F32)

    @pl.when(flags[2] == 0)
    def _():
        grid[:, :, pl.ds(0, 2), :] = jnp.zeros((4, 8, 2, 128), F32)

    @pl.when(flags[3] == 0)
    def _():
        grid[:, :, pl.ds(6, 2), :] = jnp.zeros((4, 8, 2, 128), F32)

    @pl.when(flags[4] == 0)
    def _():
        grid[0] = jnp.zeros((8, 8, 128), F32)

    @pl.when(flags[5] == 0)
    def _():
        grid[3] = jnp.zeros((8, 8, 128), F32)

    odd_row = jnp.bitwise_and(lax.broadcasted_iota(jnp.int32, (8, 128), 0), 1) == 1
    for oy in range(7):
        for x in range(8):
            for hb in range(3):
                begin = min(max(oy - 1, 0), 4)
                both = jnp.concatenate(
                    [grid[hb, x, pl.ds(begin, 4), :], grid[hb + 1, x, pl.ds(begin, 4), :]], axis=0
                )
                if oy == 0:
                    both = jnp.where(odd_row, pltpu.roll(both, 1, 0), 0.0)
                elif oy == 6:
                    both = jnp.where(odd_row, 0.0, pltpu.roll(both, 7, 0))
                first = both.astype(BF16)
                left[0, x, :, pl.ds(oy * 384 + hb * 128, 128)] = first.astype(F32)
                left[1, x, :, pl.ds(oy * 384 + hb * 128, 128)] = both - first.astype(F32)

    inner_rows = jnp.concatenate([inner[...], jnp.zeros((5, 64), F32)], axis=0)
    inner_cols = jnp.transpose(inner_rows)
    diff = [
        jnp.concatenate([inner[d : d + 1, :], inner[d : d + 1, :]], axis=1) - jnp.broadcast_to(inner_cols[:, d : d + 1], (64, 128))
        for d in range(3)
    ]
    wide = lanes((64, 128))
    right = jnp.where(wide >= 64, 1.0, 0.0)
    zsq = []
    for sz in range(6):
        offset = float(sz - 2) - right
        gap = diff[2] - offset
        zsq.append(gap * gap + SOFTEN)
    check = [None] * 4

    def over_x(ox, xs, rows):
        gap_x = diff[0] - float(ox)
        xsq = gap_x * gap_x
        for oy in range(-3, 4):
            gap_y = diff[1] - float(oy)
            xysq = xsq + gap_y * gap_y
            for sz in range(6):
                value = lax.rsqrt(xysq + zsq[sz])
                if max(abs(ox), abs(oy)) < 2:
                    left_near = abs(sz - 2) < 2
                    right_near = abs(sz - 3) < 2
                    if left_near:
                        value = jnp.where(wide < 64, 0.0, value)
                    if right_near:
                        value = jnp.where(wide >= 64, 0.0, value)
                first = value.astype(BF16)
                at = pl.ds((oy + 3) * 384 + sz * 64, 64)
                weights[at, pl.ds(0, 128)] = first
                weights[at, pl.ds(128, 128)] = (value - first.astype(F32)).astype(BF16)
        m = 8 * len(xs)
        lhs = jnp.concatenate([left[p, x] for p in range(2) for x in rows], axis=0).astype(BF16)
        prod = jnp.dot(lhs, weights[...], preferred_element_type=F32)
        part = prod[:m, :128] + prod[:m, 128:] + prod[m:, :128]
        for i, x in enumerate(xs):
            piece = part[8 * i : 8 * i + 8]
            check[x] = piece if check[x] is None else check[x] + piece

    for ox in range(-3, 4):
        if ox == -3:
            xs = (1, 3)
        elif ox == 3:
            xs = (0, 2)
        else:
            xs = (0, 1, 2, 3)
        over_x(ox, xs, [x + ox + 2 for x in xs])
    down = check_to_local(jnp.concatenate(check, axis=0), down_inv)

    for c in copies:
        c.wait()
    lane4 = lanes((4, 128))
    total[...] = before[...]
    for side, msg in enumerate((zlo, zhi)):
        sz = -1 if side == 0 else 4
        far_z = 3 if side == 0 else 0
        for ey in range(6):
            lst = side * 6 + ey
            end = jnp.int32(0)
            ends[lst * 7] = end
            for ex in range(6):
                group = 3 if ey == 0 else (6 if ey == 5 else 0)
                y = 3 if ey == 0 else (0 if ey == 5 else ey - 1)
                if ex == 0:
                    count = row_counts[side, group + 1, 4 * y + far_z].astype(jnp.int32) * flags[0]
                elif ex == 5:
                    count = row_counts[side, group + 2, 4 * y + far_z].astype(jnp.int32) * flags[1]
                else:
                    count = row_counts[side, group, 16 * (ex - 1) + 4 * y + far_z].astype(jnp.int32)
                if ey == 0:
                    count = count * flags[2]
                elif ey == 5:
                    count = count * flags[3]
                count = count * flags[4 + side]
                leaf = msg[pl.ds(64 + 4 * (6 * ex + ey), 4), :]
                end = add_source(packed, lst * 10, end, leaf, count, (float(ex - 1), float(ey - 1), float(sz)), lane4)
                ends[lst * 7 + ex + 1] = end
            close_list(packed, lst * 10, end)

    outer_columns = jnp.transpose(jnp.concatenate([outer[...], jnp.zeros((5, 64), F32)], axis=0))
    for d in range(3):
        outer_b[d] = jnp.broadcast_to(outer_columns[:, d : d + 1], (64, 128))
    rest = jnp.transpose(down)
    parts = []
    for _ in range(3):
        part = rest.astype(BF16)
        parts.append(part)
        rest = rest - part.astype(F32)
    local[...] = jnp.concatenate(parts, axis=1)
    place_of = jnp.bitwise_and(lax.broadcasted_iota(jnp.int32, (96, 128), 0), 31)

    def far_step(k, carry):
        row = jnp.right_shift(k, 2) * 8 + jnp.bitwise_and(k, 3)
        pick = jnp.concatenate(
            [jnp.where(place_of == row + 4 * hz, 1.0, 0.0).astype(BF16) for hz in range(2)], axis=1
        )
        weights_of = jnp.dot(local[...], pick, preferred_element_type=F32)
        points = [point_rows(pos, 4 * k + z) for z in range(4)]
        made = []
        for z, p in enumerate(points):
            square = SOFTEN
            for d in range(3):
                gap = p[d : d + 1] - outer_b[d]
                square = square + gap * gap
            weight = weights_of[64 * (z % 2) : 64 * (z % 2) + 64, 128 * (z // 2) : 128 * (z // 2) + 128]
            made.append(jnp.sum(lax.rsqrt(square) * weight, axis=0, keepdims=True))
        for z, value in enumerate(made):
            far[pl.ds(4 * k + z, 1), :] = value
        return carry

    lax.fori_loop(0, 16, far_step, 0)

    def leaf_of(i):
        return jnp.right_shift(i, 1) * 4 + 3 * jnp.bitwise_and(i, 1)

    spread_targets(pos, spread, turned, leaf_of, 32)

    def leaf_step(i, carry):
        side = jnp.bitwise_and(i, 1)
        n = leaf_of(i)
        x, y, z = cell_of(n)
        segments = []
        for dy in range(3):
            lst = side * 6 + y + dy
            segments.append((lst * 10, ends[lst * 7 + x], ends[lst * 7 + x + 3]))
        near_sums(i, counts[n], spread, sums, packed, segments)
        return carry

    lax.fori_loop(0, 32, leaf_step, 0)
    gather_sums(sums, total, leaf_of, 32)
    row = lax.broadcasted_iota(jnp.int32, (64, 1), 0)
    full = jnp.zeros((64, 1), jnp.int32)
    for n in range(64):
        full = jnp.where(row == n, counts[n], full)
    live = lanes((64, 128)) < full
    own_term = lax.rsqrt(jnp.full((64, 128), SOFTEN, F32))
    out[...] = jnp.where(live, jnp.transpose(total[...])[:64] + far[...] - own_term * charges[...], 0.0)


def check_to_local(check, down_inv):
    flat = jnp.transpose(down_inv[...])
    zero = jnp.zeros((64, 64), F32)
    block = jnp.concatenate(
        [jnp.concatenate([flat, zero], axis=1), jnp.concatenate([zero, flat], axis=1)], axis=0
    )
    return dot(check, block)


def final(counts, flags, pos, charges, zup, zdn, zlo, zhi, before, inner, outer, down_inv):
    return pl.pallas_call(
        final_kernel,
        out_shape=jax.ShapeDtypeStruct((64, 128), F32),
        in_specs=[pl.BlockSpec(memory_space=SMEM)] * 2 + [pl.BlockSpec(memory_space=VMEM)] * 10,
        scratch_shapes=[
            VMEM((12 * 10, 8, 128), F32),
            VMEM((32, 3, 128, 128), F32),
            VMEM((384, 192), BF16),
            VMEM((32, 128, 128), F32),
            SMEM((84,), jnp.int32),
            SMEM((2, 16, 128), F32),
            VMEM((128, 128), F32),
            VMEM((4, 8, 8, 128), F32),
            VMEM((2688, 256), BF16),
            VMEM((2, 8, 8, 2688), F32),
            VMEM((128, 96), BF16),
            VMEM((64, 128), F32),
            VMEM((3, 64, 128), F32),
            pltpu.SemaphoreType.DMA((2,)),
        ],
        compiler_params=pltpu.CompilerParams(vmem_limit_bytes=20 * 1024 * 1024),
        name="final",
    )(counts, flags, pos, charges, zup, zdn, zlo, zhi, before, inner, outer, down_inv)


def exchange(up, down, dimension):
    return (
        lax.ppermute(up, AXES, shifted(dimension, 1)),
        lax.ppermute(down, AXES, shifted(dimension, -1)),
    )


def per_device(positions, charges, counts, up_inverse, down_inverse, inner_surface, outer_surface):
    device = (lax.axis_index("gx") * 4 + lax.axis_index("gy")) * 16 + lax.axis_index("gz")
    sides = []
    for d in range(3):
        at = jnp.zeros((), jnp.int32)
        for k, b in enumerate(BITS[d]):
            at = at + jnp.left_shift(jnp.bitwise_and(jnp.right_shift(device, b), 1), k)
        sides += [at > 0, at < EXTENT[d] - 1]
    flags = jnp.stack(sides).astype(jnp.int32)
    positions = jnp.transpose(positions, (1, 0, 2))
    own, xup, xdn = upward(counts, positions, charges, outer_surface, up_inverse)
    xlo, xhi = exchange(xup, xdn, 0)
    near = near_xy((1, 2), counts, positions, charges)
    yup, ydn = pack_y(counts, positions, charges, own, xlo, xhi, near)
    ylo, yhi = exchange(yup, ydn, 1)
    near = near_xy((0, 3), counts, positions, charges, (flags, xlo, xhi, near))
    zup, zdn = pack_z(counts, positions, charges, own, xlo, xhi, yup, ylo, yhi, near)
    zlo, zhi = exchange(zup, zdn, 2)
    near = near_y(counts, flags, positions, ylo, yhi, near)
    return final(
        counts, flags, positions, charges, zup, zdn, zlo, zhi, near, inner_surface, outer_surface, down_inverse
    )


def solution(mesh):
    split = AXES
    return jax.shard_map(
        per_device,
        mesh=mesh,
        in_specs=(P(split, None, None), P(split, None), P(split), P(), P(), P(), P()),
        out_specs=P(split, None),
        check_vma=False,
    )
```

```python
import jax
import jax.numpy as jnp
from jax import lax
from jax.experimental import pallas as pl
from jax.experimental.pallas import tpu as pltpu
from jax.sharding import PartitionSpec as P

SOFTEN = 0.0025
HIGH = lax.Precision.HIGHEST
AXES = ("gx", "gy", "gz")
BITS = ((0, 3, 6), (1, 4, 7), (2, 5))
EXTENT = (8, 8, 4)
F32 = jnp.float32
BF16 = jnp.bfloat16
VMEM = pltpu.VMEM
SMEM = pltpu.SMEM
X_ROWS = 88
Y_ROWS = 136
Z_ROWS = 224


def place(q):
    return [sum(((q >> b) & 1) << k for k, b in enumerate(BITS[d])) for d in range(3)]


def linear(c):
    return sum(((c[d] >> k) & 1) << b for d in range(3) for k, b in enumerate(BITS[d]))


def shifted(dimension, step):
    pairs = []
    for q in range(256):
        c = place(q)
        c[dimension] = (c[dimension] + step) % EXTENT[dimension]
        pairs.append((q, linear(c)))
    return pairs


def lanes(shape):
    return lax.broadcasted_iota(jnp.int32, shape, len(shape) - 1)


def point_rows(pos, n):
    return jnp.concatenate([pos[d, pl.ds(n, 1), :] for d in range(3)], axis=0)


def dot(a, b):
    return jnp.dot(a, b, precision=HIGH, preferred_element_type=F32)


def upward_kernel(counts, pos, charges, outer, up_inv, own, xup, xdn, outer_b, source, density):
    oc = jnp.transpose(jnp.concatenate([outer[...], jnp.zeros((5, 64), F32)], axis=0))
    for d in range(3):
        outer_b[d] = jnp.broadcast_to(oc[:, d : d + 1], (64, 128))
    lane = lanes((1, 128))

    lane8 = lanes((64, 128))
    ones = jnp.ones((384, 128), BF16)

    def step(k, check):
        at = [8 * k + u for u in range(8)]
        loaded = [(point_rows(pos, n), charges[pl.ds(n, 1), :], counts[n]) for n in at]
        charge_rows, values = [], []
        for p, charge, count in loaded:
            q = jnp.where(lane < count, charge, 0.0)
            square = SOFTEN
            for d in range(3):
                spread = outer_b[d] - p[d : d + 1]
                square = square + spread * spread
            charge_rows.append(q)
            values.append(lax.rsqrt(square) * q)
        rest = jnp.concatenate(values[:4], axis=0)
        parts = []
        for _ in range(3):
            part = rest.astype(BF16)
            parts.append(part)
            rest = rest - part.astype(F32)
        column = jnp.dot(jnp.concatenate(parts, axis=1), ones, preferred_element_type=F32)
        columns = [column[64 * u : 64 * (u + 1)] for u in range(4)]
        columns += [jnp.sum(value, axis=1, keepdims=True) for value in values[4:]]
        for n, column in zip(at, columns):
            check = jnp.where(lane8 == n, column, check)
        for n, q in zip(at, charge_rows):
            source[pl.ds(n, 1), :] = q
        return check

    check = lax.fori_loop(0, 8, step, jnp.zeros((64, 128), F32))
    dens = jnp.transpose(dot(up_inv[...], check))[:64]
    density[...] = jnp.concatenate([dens, dens], axis=1)
    for hz in range(2):
        even = density[pl.ds(2 * hz, 16, stride=4), :]
        odd = density[pl.ds(2 * hz + 1, 16, stride=4), :]
        own[pl.ds(16 * hz, 16), :] = jnp.where(lane < 64, even, odd)
    for msg, x, xl in ((xup, 3, 2), (xdn, 0, 0)):
        for hz in range(2):
            msg[pl.ds(8 * hz, 8), :] = own[pl.ds(16 * hz + 4 * xl, 8), :]
        row = jnp.zeros((1, 128), F32)
        for k in range(16):
            n = 16 * x + k
            msg[pl.ds(16 + 4 * k, 3), :] = point_rows(pos, n)
            msg[pl.ds(16 + 4 * k + 3, 1), :] = source[pl.ds(n, 1), :]
            row = jnp.where(lane == k, counts[n].astype(F32), row)
        msg[pl.ds(80, 8), :] = jnp.broadcast_to(row, (8, 128))


def upward(counts, pos, charges, outer, up_inv):
    return pl.pallas_call(
        upward_kernel,
        out_shape=(
            jax.ShapeDtypeStruct((32, 128), F32),
            jax.ShapeDtypeStruct((X_ROWS, 128), F32),
            jax.ShapeDtypeStruct((X_ROWS, 128), F32),
        ),
        in_specs=[pl.BlockSpec(memory_space=SMEM)] + [pl.BlockSpec(memory_space=VMEM)] * 4,
        scratch_shapes=[VMEM((3, 64, 128), F32), VMEM((64, 128), F32), VMEM((64, 128), F32)],
        name="upward",
    )(counts, pos, charges, outer, up_inv)


def own_points(msg, at, pos, charges, counts, n):
    msg[pl.ds(at, 3), :] = point_rows(pos, n)
    msg[pl.ds(at + 3, 1), :] = jnp.where(lanes((1, 128)) < counts[n], charges[pl.ds(n, 1), :], 0.0)


def pack_y_kernel(counts, pos, charges, own, xlo, xhi, near, yup, ydn):
    lane = lanes((1, 128))
    row = jnp.zeros((1, 128), F32)
    for k in range(64):
        row = jnp.where(lane == k, counts[k].astype(F32), row)
    for msg, y, yl in ((yup, 3, 2), (ydn, 0, 0)):
        for hz in range(2):
            for ex in range(8):
                at = pl.ds((hz * 8 + ex) * 2, 2)
                if ex < 2:
                    msg[at, :] = xlo[pl.ds((hz * 2 + ex) * 4 + yl, 2), :]
                elif ex < 6:
                    msg[at, :] = own[pl.ds((hz * 4 + ex - 2) * 4 + yl, 2), :]
                else:
                    msg[at, :] = xhi[pl.ds((hz * 2 + ex - 6) * 4 + yl, 2), :]
        for z in range(4):
            msg[pl.ds(32 + 4 * z, 4), :] = xlo[pl.ds(16 + 4 * (4 * y + z), 4), :]
            for x in range(4):
                own_points(msg, 32 + 4 * (4 * (x + 1) + z), pos, charges, counts, 16 * x + 4 * y + z)
            msg[pl.ds(32 + 4 * (20 + z), 4), :] = xhi[pl.ds(16 + 4 * (4 * y + z), 4), :]
        msg[pl.ds(128, 1), :] = row
        msg[pl.ds(129, 1), :] = xlo[pl.ds(80, 1), :]
        msg[pl.ds(130, 1), :] = xhi[pl.ds(80, 1), :]
        msg[pl.ds(131, 5), :] = jnp.zeros((5, 128), F32)


def pack_y(counts, pos, charges, own, xlo, xhi, near):
    return pl.pallas_call(
        pack_y_kernel,
        out_shape=(jax.ShapeDtypeStruct((Y_ROWS, 128), F32),) * 2,
        in_specs=[pl.BlockSpec(memory_space=SMEM)] + [pl.BlockSpec(memory_space=VMEM)] * 5 + [pl.BlockSpec(memory_space=pl.ANY)],
        compiler_params=pltpu.CompilerParams(vmem_limit_bytes=6 * 1024 * 1024),
        name="pack_y",
    )(counts, pos, charges, own, xlo, xhi, near)


def pack_z_kernel(counts, pos, charges, own, xlo, xhi, yup, ylo, yhi, near, zup, zdn):
    for msg, z, hz in ((zup, 3, 1), (zdn, 0, 0)):
        for ex in range(8):
            at = ex * 8
            msg[pl.ds(at, 2), :] = ylo[pl.ds((hz * 8 + ex) * 2, 2), :]
            if ex < 2:
                msg[pl.ds(at + 2, 4), :] = xlo[pl.ds((hz * 2 + ex) * 4, 4), :]
            elif ex < 6:
                msg[pl.ds(at + 2, 4), :] = own[pl.ds((hz * 4 + ex - 2) * 4, 4), :]
            else:
                msg[pl.ds(at + 2, 4), :] = xhi[pl.ds((hz * 2 + ex - 6) * 4, 4), :]
            msg[pl.ds(at + 6, 2), :] = yhi[pl.ds((hz * 8 + ex) * 2, 2), :]
        for ex in range(6):
            for ey in range(6):
                at = 64 + 4 * (6 * ex + ey)
                if ey == 0:
                    msg[pl.ds(at, 4), :] = ylo[pl.ds(32 + 4 * (4 * ex + z), 4), :]
                elif ey == 5:
                    msg[pl.ds(at, 4), :] = yhi[pl.ds(32 + 4 * (4 * ex + z), 4), :]
                elif ex == 0:
                    msg[pl.ds(at, 4), :] = xlo[pl.ds(16 + 4 * (4 * (ey - 1) + z), 4), :]
                elif ex == 5:
                    msg[pl.ds(at, 4), :] = xhi[pl.ds(16 + 4 * (4 * (ey - 1) + z), 4), :]
                else:
                    own_points(msg, at, pos, charges, counts, 16 * (ex - 1) + 4 * (ey - 1) + z)
        msg[pl.ds(208, 3), :] = yup[pl.ds(128, 3), :]
        msg[pl.ds(211, 3), :] = ylo[pl.ds(128, 3), :]
        msg[pl.ds(214, 3), :] = yhi[pl.ds(128, 3), :]
        msg[pl.ds(217, 7), :] = jnp.zeros((7, 128), F32)


def pack_z(counts, pos, charges, own, xlo, xhi, yup, ylo, yhi, near):
    return pl.pallas_call(
        pack_z_kernel,
        out_shape=(jax.ShapeDtypeStruct((Z_ROWS, 128), F32),) * 2,
        in_specs=[pl.BlockSpec(memory_space=SMEM)] + [pl.BlockSpec(memory_space=VMEM)] * 8 + [pl.BlockSpec(memory_space=pl.ANY)],
        compiler_params=pltpu.CompilerParams(vmem_limit_bytes=6 * 1024 * 1024),
        name="pack_z",
    )(counts, pos, charges, own, xlo, xhi, yup, ylo, yhi, near)


def add_source(packed, base, place_at, leaf, count, cell, lane):
    off = jnp.bitwise_and(place_at, 127)
    tile = base + jnp.right_shift(place_at, 7)
    row = lax.broadcasted_iota(jnp.int32, (4, 128), 0)
    shift = jnp.where(row == 0, cell[0], jnp.where(row == 1, cell[1], jnp.where(row == 2, cell[2], 0.0)))
    rolled = pltpu.roll(leaf + shift, off, 1)
    packed[tile, pl.ds(0, 4), :] = jnp.where(lane >= off, rolled, packed[tile, pl.ds(0, 4), :])
    packed[tile + 1, pl.ds(0, 4), :] = rolled
    return place_at + count


def close_list(packed, base, end):
    packed[base + jnp.right_shift(end, 7) + 1, pl.ds(0, 4), :] = jnp.zeros((4, 128), F32)
    packed[base + jnp.right_shift(end, 7) + 2, pl.ds(0, 4), :] = jnp.zeros((4, 128), F32)


def cell_of(n):
    return jnp.right_shift(n, 4), jnp.bitwise_and(jnp.right_shift(n, 2), 3), jnp.bitwise_and(n, 3)


def spread_targets(pos, spread, turned, leaf_of, leaves):
    number = lax.broadcasted_iota(jnp.int32, (64, 128), 0)
    for d, part in enumerate(cell_of(number)):
        flat = pos[d] + part.astype(F32)
        rest = jnp.transpose(jnp.concatenate([flat, flat], axis=0))[:, :64]
        for p in range(3):
            piece = rest.astype(BF16)
            turned[pl.ds(128 * d, 128), pl.ds(64 * p, 64)] = piece
            rest = rest - piece.astype(F32)
    place_of = jnp.bitwise_and(lax.broadcasted_iota(jnp.int32, (192, 128), 0), 63)

    def step(k, carry):
        pick = jnp.concatenate(
            [jnp.where(place_of == leaf_of(8 * k + u), 1.0, 0.0).astype(BF16) for u in range(8)], axis=1
        )
        wide = jnp.dot(turned[...], pick, preferred_element_type=F32)
        for u in range(8):
            for d in range(3):
                spread[8 * k + u, d] = wide[128 * d : 128 * (d + 1), 128 * u : 128 * (u + 1)]
        return carry

    lax.fori_loop(0, leaves // 8, step, 0)


TOGETHER = ((1, 4), (2, 2), (3, 2), (4, 1))


def near_sums(i, count, spread, sums, packed, segments):
    lane = lanes((1, 128))
    shifts, starts, stops, upto = [], [], [], []
    have = jnp.int32(0)
    for base, start, stop in segments:
        first = jnp.right_shift(start, 7)
        number = jnp.where(stop > start, jnp.right_shift(stop + 127, 7) - first, 0)
        shifts.append(base + first - have)
        starts.append(base * 128 + start)
        stops.append(base * 128 + stop)
        have = have + number
        upto.append(have)

    def pick(values, tests):
        value = values[-1]
        for k in range(len(values) - 2, -1, -1):
            value = jnp.where(tests[k], values[k], value)
        return value

    def run(groups, together):
        rows = pl.ds(0, 8 * groups)
        blocks = lax.div(have + together - 1, together)

        def where_is(b):
            found = []
            for u in range(together):
                j = b * together + u
                inside = jnp.maximum(jnp.minimum(j, have - 1), 0)
                tests = [inside < end for end in upto[:-1]]
                tile = pick(shifts, tests) + inside
                stop = jnp.where(j < have, pick(stops, tests), 0)
                found.append((tile, pick(starts, tests) - tile * 128, stop - tile * 128))
            return found

        def ahead(found):
            squares, charges = [], []
            for tile, low, high in found:
                keep = (lane >= low) & (lane < high)
                charges.append(jnp.where(keep, packed[tile, pl.ds(3, 1), :], 0.0))
                square = SOFTEN
                for d in range(3):
                    gap = spread[i, d, rows, :] - packed[tile, pl.ds(d, 1), :]
                    square = square + gap * gap
                squares.append(square)
            return squares, charges

        def add(acc, squares, charges):
            roots = [lax.rsqrt(square) for square in squares]
            for root, charge in zip(roots, charges):
                acc = acc + root * charge
            return acc

        def step(b, carry):
            acc, squares, charges, found = carry
            acc = add(acc, squares, charges)
            return (acc, *ahead(found), where_is(b + 1))

        begin = jnp.zeros((8 * groups, 128), F32)
        acc, squares, charges, _ = lax.fori_loop(1, blocks, step, (begin, *ahead(where_is(0)), where_is(1)))
        sums[i, rows, :] = add(acc, squares, charges)

    size = jnp.right_shift(count + 31, 5)
    for k, together in TOGETHER:

        @pl.when(size == k)
        def _():
            run(4 * k, together)


def gather_sums(sums, total, leaf_of, leaves):
    wide = lanes((128, 128))
    ones = jnp.ones((256, 128), BF16)

    def step(k, carry):
        value = jnp.concatenate([sums[8 * k + u] for u in range(4)], axis=0)
        first = value.astype(BF16)
        second = (value - first.astype(F32)).astype(BF16)
        column = jnp.dot(jnp.concatenate([first, second], axis=1), ones, preferred_element_type=F32)
        columns = [column[128 * u : 128 * (u + 1)] for u in range(4)]
        columns += [jnp.sum(sums[8 * k + u], axis=1, keepdims=True) for u in range(4, 8)]
        for u, column in enumerate(columns):
            carry = jnp.where(wide == leaf_of(8 * k + u), carry + column, carry)
        return carry

    total[...] = lax.fori_loop(0, leaves // 8, step, total[...])


def near_xy_kernel(windows, *refs):
    if len(refs) == 10:
        counts, pos, charges, total, packed, spread, turned, sums, ends, _ = refs
        xlo = xhi = None
    else:
        counts, flags, pos, charges, xlo, xhi, before, total, packed, spread, turned, sums, ends, lo_counts, hi_counts, sem = refs
        a = pltpu.make_async_copy(xlo.at[pl.ds(80, 1), :], lo_counts, sem.at[0])
        b = pltpu.make_async_copy(xhi.at[pl.ds(80, 1), :], hi_counts, sem.at[1])
        a.start()
        b.start()
        a.wait()
        b.wait()
    lane4 = lanes((4, 128))
    lane = lanes((1, 128))
    total[...] = jnp.zeros((128, 128), F32) if xlo is None else before[...]
    for w, x in enumerate(windows):
        for z in range(4):
            base = (w * 4 + z) * 16
            end = jnp.int32(0)
            ends[(w * 4 + z) * 5] = end
            for y in range(4):
                for dx in (-1, 0, 1):
                    sx = x + dx
                    k = 4 * y + z
                    cell = (float(sx), float(y), float(z))
                    if 0 <= sx < 4:
                        n = 16 * sx + k
                        count = counts[n]
                        q = jnp.where(lane < count, charges[pl.ds(n, 1), :], 0.0)
                        leaf = jnp.concatenate([point_rows(pos, n), q], axis=0)
                    else:
                        msg, cnt, flag = (xlo, lo_counts, 0) if sx < 0 else (xhi, hi_counts, 1)
                        count = cnt[0, k].astype(jnp.int32) * flags[flag]
                        leaf = msg[pl.ds(16 + 4 * k, 4), :]
                    end = add_source(packed, base, end, leaf, count, cell, lane4)
                ends[(w * 4 + z) * 5 + y + 1] = end
            close_list(packed, base, end)

    def leaf_of(i):
        return jnp.bitwise_and(i, 15) + 16 * (windows[0] + jnp.right_shift(i, 4) * (windows[1] - windows[0]))

    spread_targets(pos, spread, turned, leaf_of, 32)

    def leaf_step(i, carry):
        w = jnp.right_shift(i, 4)
        n = leaf_of(i)
        x, y, z = cell_of(n)
        segments = []
        for dz in (-1, 0, 1):
            zz = jnp.clip(z + dz, 0, 3)
            lst = w * 4 + zz
            start = ends[lst * 5 + jnp.maximum(y - 1, 0)]
            stop = ends[lst * 5 + jnp.minimum(y + 1, 3) + 1]
            if dz:
                stop = jnp.where(zz == z + dz, stop, start)
            segments.append((lst * 16, start, stop))
        near_sums(i, counts[n], spread, sums, packed, segments)
        return carry

    lax.fori_loop(0, 32, leaf_step, 0)
    gather_sums(sums, total, leaf_of, 32)


def near_xy(windows, counts, pos, charges, halo=None):
    call_args = [counts, pos, charges]
    specs = [pl.BlockSpec(memory_space=SMEM)] + [pl.BlockSpec(memory_space=VMEM)] * 2
    if halo is not None:
        flags, xlo, xhi, before = halo
        call_args = [counts, flags, pos, charges, xlo, xhi, before]
        specs = [pl.BlockSpec(memory_space=SMEM)] * 2 + [pl.BlockSpec(memory_space=VMEM)] * 5
    scratch = [
        VMEM((8 * 16, 8, 128), F32),
        VMEM((32, 3, 128, 128), F32),
            VMEM((384, 192), BF16),
        VMEM((32, 128, 128), F32),
        SMEM((40,), jnp.int32),
        SMEM((1, 128), F32),
    ]
    if halo is not None:
        scratch += [SMEM((1, 128), F32), pltpu.SemaphoreType.DMA((2,))]

    def body(*refs):
        near_xy_kernel(windows, *refs)

    return pl.pallas_call(
        body,
        out_shape=jax.ShapeDtypeStruct((128, 128), F32),
        in_specs=specs,
        scratch_shapes=scratch,
        compiler_params=pltpu.CompilerParams(vmem_limit_bytes=14 * 1024 * 1024),
        cost_estimate=pl.CostEstimate(flops=150_000_000, bytes_accessed=300_000, transcendentals=10_000_000),
        name="near_x",
    )(*call_args)


def near_y_kernel(counts, flags, pos, ylo, yhi, before, total, packed, spread, turned, sums, ends, row_counts, sem):
    copies = [
        pltpu.make_async_copy(msg.at[pl.ds(128, 8), :], row_counts.at[i], sem.at[i])
        for i, msg in enumerate((ylo, yhi))
    ]
    for c in copies:
        c.start()
    for c in copies:
        c.wait()
    lane4 = lanes((4, 128))
    total[...] = before[...]
    for side, msg in enumerate((ylo, yhi)):
        sy = -1 if side == 0 else 4
        far_y = 3 if side == 0 else 0
        for z in range(4):
            lst = side * 4 + z
            end = jnp.int32(0)
            ends[lst * 7] = end
            for ex in range(6):
                if ex == 0:
                    count = row_counts[side, 1, 4 * far_y + z].astype(jnp.int32) * flags[0]
                elif ex == 5:
                    count = row_counts[side, 2, 4 * far_y + z].astype(jnp.int32) * flags[1]
                else:
                    count = row_counts[side, 0, 16 * (ex - 1) + 4 * far_y + z].astype(jnp.int32)
                count = count * flags[2 + side]
                leaf = msg[pl.ds(32 + 4 * (4 * ex + z), 4), :]
                end = add_source(packed, lst * 10, end, leaf, count, (float(ex - 1), float(sy), float(z)), lane4)
                ends[lst * 7 + ex + 1] = end
            close_list(packed, lst * 10, end)

    def leaf_of(i):
        side = jnp.right_shift(i, 4)
        x = jnp.bitwise_and(jnp.right_shift(i, 2), 3)
        return 16 * x + 12 * side + jnp.bitwise_and(i, 3)

    spread_targets(pos, spread, turned, leaf_of, 32)

    def leaf_step(i, carry):
        side = jnp.right_shift(i, 4)
        n = leaf_of(i)
        x, y, z = cell_of(n)
        segments = []
        for dz in (-1, 0, 1):
            zz = jnp.clip(z + dz, 0, 3)
            lst = side * 4 + zz
            start = ends[lst * 7 + x]
            stop = ends[lst * 7 + x + 3]
            if dz:
                stop = jnp.where(zz == z + dz, stop, start)
            segments.append((lst * 10, start, stop))
        near_sums(i, counts[n], spread, sums, packed, segments)
        return carry

    lax.fori_loop(0, 32, leaf_step, 0)
    gather_sums(sums, total, leaf_of, 32)


def near_y(counts, flags, pos, ylo, yhi, before):
    return pl.pallas_call(
        near_y_kernel,
        out_shape=jax.ShapeDtypeStruct((128, 128), F32),
        in_specs=[pl.BlockSpec(memory_space=SMEM)] * 2 + [pl.BlockSpec(memory_space=VMEM)] * 4,
        scratch_shapes=[
            VMEM((8 * 10, 8, 128), F32),
            VMEM((32, 3, 128, 128), F32),
            VMEM((384, 192), BF16),
            VMEM((32, 128, 128), F32),
            SMEM((56,), jnp.int32),
            SMEM((2, 8, 128), F32),
            pltpu.SemaphoreType.DMA((2,)),
        ],
        compiler_params=pltpu.CompilerParams(vmem_limit_bytes=14 * 1024 * 1024),
        cost_estimate=pl.CostEstimate(flops=60_000_000, bytes_accessed=300_000, transcendentals=4_000_000),
        name="near_y",
    )(counts, flags, pos, ylo, yhi, before)


def final_kernel(
    counts, flags, pos, charges, zup, zdn, zlo, zhi, before, inner, outer, down_inv,
    out, packed, spread, turned, sums, ends, row_counts, total, grid, weights, left, local, far, outer_b, sem,
):
    copies = [
        pltpu.make_async_copy(msg.at[pl.ds(208, 16), :], row_counts.at[i], sem.at[i])
        for i, msg in enumerate((zlo, zhi))
    ]
    for c in copies:
        c.start()
    grid[1] = zdn[pl.ds(0, 64), :].reshape(8, 8, 128)
    grid[2] = zup[pl.ds(0, 64), :].reshape(8, 8, 128)
    grid[0] = zlo[pl.ds(0, 64), :].reshape(8, 8, 128)
    grid[3] = zhi[pl.ds(0, 64), :].reshape(8, 8, 128)

    @pl.when(flags[0] == 0)
    def _():
        grid[:, pl.ds(0, 2)] = jnp.zeros((4, 2, 8, 128), F32)

    @pl.when(flags[1] == 0)
    def _():
        grid[:, pl.ds(6, 2)] = jnp.zeros((4, 2, 8, 128), F32)

    @pl.when(flags[2] == 0)
    def _():
        grid[:, :, pl.ds(0, 2), :] = jnp.zeros((4, 8, 2, 128), F32)

    @pl.when(flags[3] == 0)
    def _():
        grid[:, :, pl.ds(6, 2), :] = jnp.zeros((4, 8, 2, 128), F32)

    @pl.when(flags[4] == 0)
    def _():
        grid[0] = jnp.zeros((8, 8, 128), F32)

    @pl.when(flags[5] == 0)
    def _():
        grid[3] = jnp.zeros((8, 8, 128), F32)

    odd_row = jnp.bitwise_and(lax.broadcasted_iota(jnp.int32, (8, 128), 0), 1) == 1
    for oy in range(7):
        for x in range(8):
            for hb in range(3):
                begin = min(max(oy - 1, 0), 4)
                both = jnp.concatenate(
                    [grid[hb, x, pl.ds(begin, 4), :], grid[hb + 1, x, pl.ds(begin, 4), :]], axis=0
                )
                if oy == 0:
                    both = jnp.where(odd_row, pltpu.roll(both, 1, 0), 0.0)
                elif oy == 6:
                    both = jnp.where(odd_row, 0.0, pltpu.roll(both, 7, 0))
                first = both.astype(BF16)
                left[0, x, :, pl.ds(oy * 384 + hb * 128, 128)] = first.astype(F32)
                left[1, x, :, pl.ds(oy * 384 + hb * 128, 128)] = both - first.astype(F32)

    inner_rows = jnp.concatenate([inner[...], jnp.zeros((5, 64), F32)], axis=0)
    inner_cols = jnp.transpose(inner_rows)
    diff = [
        jnp.concatenate([inner[d : d + 1, :], inner[d : d + 1, :]], axis=1) - jnp.broadcast_to(inner_cols[:, d : d + 1], (64, 128))
        for d in range(3)
    ]
    wide = lanes((64, 128))
    right = jnp.where(wide >= 64, 1.0, 0.0)
    zsq = []
    for sz in range(6):
        offset = float(sz - 2) - right
        gap = diff[2] - offset
        zsq.append(gap * gap + SOFTEN)
    check = [None] * 4

    def over_x(ox, xs, rows):
        gap_x = diff[0] - float(ox)
        xsq = gap_x * gap_x
        for oy in range(-3, 4):
            gap_y = diff[1] - float(oy)
            xysq = xsq + gap_y * gap_y
            for sz in range(6):
                value = lax.rsqrt(xysq + zsq[sz])
                if max(abs(ox), abs(oy)) < 2:
                    left_near = abs(sz - 2) < 2
                    right_near = abs(sz - 3) < 2
                    if left_near:
                        value = jnp.where(wide < 64, 0.0, value)
                    if right_near:
                        value = jnp.where(wide >= 64, 0.0, value)
                first = value.astype(BF16)
                at = pl.ds((oy + 3) * 384 + sz * 64, 64)
                weights[at, pl.ds(0, 128)] = first
                weights[at, pl.ds(128, 128)] = (value - first.astype(F32)).astype(BF16)
        m = 8 * len(xs)
        lhs = jnp.concatenate([left[p, x] for p in range(2) for x in rows], axis=0).astype(BF16)
        prod = jnp.dot(lhs, weights[...], preferred_element_type=F32)
        part = prod[:m, :128] + prod[:m, 128:] + prod[m:, :128]
        for i, x in enumerate(xs):
            piece = part[8 * i : 8 * i + 8]
            check[x] = piece if check[x] is None else check[x] + piece

    for ox in range(-3, 4):
        if ox == -3:
            xs = (1, 3)
        elif ox == 3:
            xs = (0, 2)
        else:
            xs = (0, 1, 2, 3)
        over_x(ox, xs, [x + ox + 2 for x in xs])
    down = check_to_local(jnp.concatenate(check, axis=0), down_inv)

    for c in copies:
        c.wait()
    lane4 = lanes((4, 128))
    total[...] = before[...]
    for side, msg in enumerate((zlo, zhi)):
        sz = -1 if side == 0 else 4
        far_z = 3 if side == 0 else 0
        for ey in range(6):
            lst = side * 6 + ey
            end = jnp.int32(0)
            ends[lst * 7] = end
            for ex in range(6):
                group = 3 if ey == 0 else (6 if ey == 5 else 0)
                y = 3 if ey == 0 else (0 if ey == 5 else ey - 1)
                if ex == 0:
                    count = row_counts[side, group + 1, 4 * y + far_z].astype(jnp.int32) * flags[0]
                elif ex == 5:
                    count = row_counts[side, group + 2, 4 * y + far_z].astype(jnp.int32) * flags[1]
                else:
                    count = row_counts[side, group, 16 * (ex - 1) + 4 * y + far_z].astype(jnp.int32)
                if ey == 0:
                    count = count * flags[2]
                elif ey == 5:
                    count = count * flags[3]
                count = count * flags[4 + side]
                leaf = msg[pl.ds(64 + 4 * (6 * ex + ey), 4), :]
                end = add_source(packed, lst * 10, end, leaf, count, (float(ex - 1), float(ey - 1), float(sz)), lane4)
                ends[lst * 7 + ex + 1] = end
            close_list(packed, lst * 10, end)

    outer_columns = jnp.transpose(jnp.concatenate([outer[...], jnp.zeros((5, 64), F32)], axis=0))
    for d in range(3):
        outer_b[d] = jnp.broadcast_to(outer_columns[:, d : d + 1], (64, 128))
    rest = jnp.transpose(down)
    parts = []
    for _ in range(3):
        part = rest.astype(BF16)
        parts.append(part)
        rest = rest - part.astype(F32)
    local[...] = jnp.concatenate(parts, axis=1)
    place_of = jnp.bitwise_and(lax.broadcasted_iota(jnp.int32, (96, 128), 0), 31)

    def far_step(k, carry):
        row = jnp.right_shift(k, 2) * 8 + jnp.bitwise_and(k, 3)
        pick = jnp.concatenate(
            [jnp.where(place_of == row + 4 * hz, 1.0, 0.0).astype(BF16) for hz in range(2)], axis=1
        )
        weights_of = jnp.dot(local[...], pick, preferred_element_type=F32)
        points = [point_rows(pos, 4 * k + z) for z in range(4)]
        made = []
        for z, p in enumerate(points):
            square = SOFTEN
            for d in range(3):
                gap = p[d : d + 1] - outer_b[d]
                square = square + gap * gap
            weight = weights_of[64 * (z % 2) : 64 * (z % 2) + 64, 128 * (z // 2) : 128 * (z // 2) + 128]
            made.append(jnp.sum(lax.rsqrt(square) * weight, axis=0, keepdims=True))
        for z, value in enumerate(made):
            far[pl.ds(4 * k + z, 1), :] = value
        return carry

    lax.fori_loop(0, 16, far_step, 0)

    def leaf_of(i):
        return jnp.right_shift(i, 1) * 4 + 3 * jnp.bitwise_and(i, 1)

    spread_targets(pos, spread, turned, leaf_of, 32)

    def leaf_step(i, carry):
        side = jnp.bitwise_and(i, 1)
        n = leaf_of(i)
        x, y, z = cell_of(n)
        segments = []
        for dy in range(3):
            lst = side * 6 + y + dy
            segments.append((lst * 10, ends[lst * 7 + x], ends[lst * 7 + x + 3]))
        near_sums(i, counts[n], spread, sums, packed, segments)
        return carry

    lax.fori_loop(0, 32, leaf_step, 0)
    gather_sums(sums, total, leaf_of, 32)
    row = lax.broadcasted_iota(jnp.int32, (64, 1), 0)
    full = jnp.zeros((64, 1), jnp.int32)
    for n in range(64):
        full = jnp.where(row == n, counts[n], full)
    live = lanes((64, 128)) < full
    own_term = lax.rsqrt(jnp.full((64, 128), SOFTEN, F32))
    out[...] = jnp.where(live, jnp.transpose(total[...])[:64] + far[...] - own_term * charges[...], 0.0)


def check_to_local(check, down_inv):
    flat = jnp.transpose(down_inv[...])
    zero = jnp.zeros((64, 64), F32)
    block = jnp.concatenate(
        [jnp.concatenate([flat, zero], axis=1), jnp.concatenate([zero, flat], axis=1)], axis=0
    )
    return dot(check, block)


def final(counts, flags, pos, charges, zup, zdn, zlo, zhi, before, inner, outer, down_inv):
    return pl.pallas_call(
        final_kernel,
        out_shape=jax.ShapeDtypeStruct((64, 128), F32),
        in_specs=[pl.BlockSpec(memory_space=SMEM)] * 2 + [pl.BlockSpec(memory_space=VMEM)] * 10,
        scratch_shapes=[
            VMEM((12 * 10, 8, 128), F32),
            VMEM((32, 3, 128, 128), F32),
            VMEM((384, 192), BF16),
            VMEM((32, 128, 128), F32),
            SMEM((84,), jnp.int32),
            SMEM((2, 16, 128), F32),
            VMEM((128, 128), F32),
            VMEM((4, 8, 8, 128), F32),
            VMEM((2688, 256), BF16),
            VMEM((2, 8, 8, 2688), F32),
            VMEM((128, 96), BF16),
            VMEM((64, 128), F32),
            VMEM((3, 64, 128), F32),
            pltpu.SemaphoreType.DMA((2,)),
        ],
        compiler_params=pltpu.CompilerParams(vmem_limit_bytes=20 * 1024 * 1024),
        name="final",
    )(counts, flags, pos, charges, zup, zdn, zlo, zhi, before, inner, outer, down_inv)


def exchange(up, down, dimension):
    return (
        lax.ppermute(up, AXES, shifted(dimension, 1)),
        lax.ppermute(down, AXES, shifted(dimension, -1)),
    )


def per_device(positions, charges, counts, up_inverse, down_inverse, inner_surface, outer_surface):
    device = (lax.axis_index("gx") * 4 + lax.axis_index("gy")) * 16 + lax.axis_index("gz")
    sides = []
    for d in range(3):
        at = jnp.zeros((), jnp.int32)
        for k, b in enumerate(BITS[d]):
            at = at + jnp.left_shift(jnp.bitwise_and(jnp.right_shift(device, b), 1), k)
        sides += [at > 0, at < EXTENT[d] - 1]
    flags = jnp.stack(sides).astype(jnp.int32)
    positions = jnp.transpose(positions, (1, 0, 2))
    own, xup, xdn = upward(counts, positions, charges, outer_surface, up_inverse)
    xlo, xhi = exchange(xup, xdn, 0)
    near = near_xy((1, 2), counts, positions, charges)
    yup, ydn = pack_y(counts, positions, charges, own, xlo, xhi, near)
    ylo, yhi = exchange(yup, ydn, 1)
    near = near_xy((0, 3), counts, positions, charges, (flags, xlo, xhi, near))
    zup, zdn = pack_z(counts, positions, charges, own, xlo, xhi, yup, ylo, yhi, near)
    zlo, zhi = exchange(zup, zdn, 2)
    near = near_y(counts, flags, positions, ylo, yhi, near)
    return final(
        counts, flags, positions, charges, zup, zdn, zlo, zhi, near, inner_surface, outer_surface, down_inverse
    )


def solution(mesh):
    split = AXES
    return jax.shard_map(
        per_device,
        mesh=mesh,
        in_specs=(P(split, None, None), P(split, None), P(split), P(), P(), P(), P()),
        out_specs=P(split, None),
        check_vma=False,
    )
```
